32 devices in a mesh: section: 2 (over x), cp: 4 (over y, core), tp: 4 (over z).
Axes of the slice: x: 2, y: 2, z: 4, core: 2. Of those that a mesh axis runs over, the one named last changes fastest.
Arguments:
- rollout_rows: bfloat16 [512, 8192], P(('section', 'cp'), 'tp'), may hold values from -60 to 60
- lengths: int32 [2], replicated, may hold values from 1 to 384, 512 in all
- block_owner: int32 [8], replicated, may hold values from 0 to 7, each once
- norm_gain: float32 [2, 8192], P('section', 'tp'), may hold values from 0.1 to 1.9
- w_qkv: bfloat16 [2, 3, 8192, 8192], P('section', None, 'tp', 'cp'), may hold values from -1 to 1
- w_out: bfloat16 [2, 8192, 8192], P('section', 'cp', 'tp'), may hold values from -0.5 to 0.5
Outputs:
- scored: bfloat16 [2, 512, 8192], P(None, ('section', 'cp'), 'tp')
The draws below stay inside these ranges and needn't reach their ends.
Inputs may be any that keep to these rules, and one draw needn't show every extreme that they name: The 2 lengths sum to 512; neither is over 384. `block_owner`: every owner block appears once.
All inputs are finite; a program needn't handle non-finite values.
Results may differ from the reference program's by a relative error of at most 0.022.
Values may be sent and summed in bfloat16 or wider, within the bound.
A program may use at most 128 MiB of HBM per device.

```python
import math
import jax
import jax.numpy as jnp
import numpy as np
from jax import lax

D = 8192
HEADS = 64
HEAD = 128
NSEQ = 2
TOKENS = 512
MOST = 384
NBLK = 8
N_CP = 4


def draw_rollout_rows(key, part):
    first, second, third = jax.random.split(key, 3)
    row_scale = jnp.exp(jax.random.uniform(first, (TOKENS, 1), jnp.float32, math.log(0.3), math.log(3.0)))
    column_ramp = jnp.arange(D, dtype=jnp.float32) / D - 0.5
    column_scale = jnp.power(10.0, column_ramp) * jnp.exp(jax.random.uniform(second, (D,), jnp.float32, -0.35, 0.35))
    entries = jax.random.truncated_normal(third, -4.0, 4.0, (TOKENS, D), jnp.float32)
    return (entries * row_scale * column_scale[None, :]).astype(jnp.bfloat16)


def draw_w_qkv(key, part):
    first = jax.random.fold_in(key, 0)
    entries = jax.random.truncated_normal(first, -4.0, 4.0, (2, 3, D, HEADS, HEAD), jnp.float32) / math.sqrt(D)
    return entries.reshape(2, 3, D, HEADS * HEAD).astype(jnp.bfloat16)


def block_scale(rng, shape, cuts, low, high):
    factor_of, own = 1.0, jax.random.fold_in(rng, 6)
    for axis_at, parts in cuts:
        heights = jnp.exp(jax.random.uniform(jax.random.fold_in(own, axis_at), (parts,), jnp.float32, low / len(cuts), high / len(cuts)))
        factor_of = factor_of * jnp.repeat(heights, shape[axis_at] // parts).reshape([-1 if axis == axis_at else 1 for axis in range(len(shape))])
    return factor_of


def length_profile(number_of, total, limit, skew):
    weights = [(1 << 20) // math.isqrt(standing ** skew) + 1 for standing in range(2, number_of + 1)]
    spare, given = total - limit - (number_of - 1), [1] * (number_of - 1)
    while spare > 0:
        candidates = [i for i in range(number_of - 1) if given[i] < limit]
        whole, remaining = sum([weights[i] for i in candidates]), spare
        for i in candidates:
            extra = min(limit - given[i], max(1, remaining * weights[i] // whole), spare)
            given[i] = given[i] + extra
            spare = spare - extra
    return np.array([limit] + given)


def uneven_parts(rng, amount, total, bound, skew):
    if amount == 2:
        one = jax.random.randint(rng, (), max(1, total - bound), min(bound, total - 1) + 1)
        return jnp.stack([one, total - one])
    tallies = jnp.asarray(length_profile(amount, total, bound, skew), jnp.int32)
    twos = (amount - 1) // 2
    donor, receiver = tallies[1:1 + 2 * twos:2], tallies[2:2 + 2 * twos:2]
    room = jnp.minimum(donor - 1, bound - receiver)
    moved = jax.random.randint(jax.random.fold_in(rng, 1), (twos,), 0, 1 << 20) % (room + 1)
    tallies = tallies.at[1:1 + 2 * twos:2].set(donor - moved).at[2:2 + 2 * twos:2].set(receiver + moved)
    return tallies[jax.random.permutation(jax.random.fold_in(rng, 2), amount)]


def scatter_about(own_key, extent, width, reach, pieces=(), kind=jnp.bfloat16):
    drawn = width * jax.random.normal(own_key, extent, jnp.float32)
    if pieces:
        drawn = drawn * block_scale(own_key, extent, pieces, -0.22, 0.18)
    return jnp.clip(drawn, -reach, reach).astype(kind)


def setup_inputs(seed: int = 0) -> dict:
    streams_of = jax.random.split(jax.random.key(seed), 7)
    return {
        "rollout_rows": draw_rollout_rows(jax.random.fold_in(streams_of[6], 71), 0),
        "lengths": uneven_parts(streams_of[1], NSEQ, TOKENS, MOST, 2).astype(jnp.int32),
        "block_owner": jax.random.permutation(streams_of[2], NBLK).astype(jnp.int32),
        "norm_gain": jnp.clip(1.0 + 0.18 * jax.random.normal(streams_of[3], (2, D), jnp.float32), 0.1, 1.9),
        "w_qkv": draw_w_qkv(jax.random.fold_in(streams_of[6], 71), 0),
        "w_out": scatter_about(streams_of[5], (2, HEADS * HEAD, D), HEAD ** -0.5, 0.5, ((0, 2), (1, 4), (2, 4))),
    }


def reference(rollout_rows, lengths, block_owner, norm_gain, w_qkv, w_out):
    own_rows = TOKENS // NBLK
    packed = rollout_rows.reshape(NBLK, own_rows, D)[block_owner].reshape(TOKENS, D)
    position = jnp.arange(TOKENS, dtype=jnp.int32)
    seq_ends = jnp.cumsum(lengths).astype(jnp.int32)
    sequence = lax.optimization_barrier(jnp.sum((position[:, None] >= seq_ends[None, :]).astype(jnp.int32), axis=1))
    allowed = (sequence[:, None] == sequence[None, :]) & (position[None, :] <= position[:, None])
    mean_square = lax.optimization_barrier(jnp.mean(jnp.square(packed.astype(jnp.float32)), axis=1, keepdims=True))
    inverse_rms = lax.rsqrt(mean_square + 1e-05)
    group_width = HEADS * HEAD // N_CP
    outputs = []
    for model_index in range(2):
        normed = (packed.astype(jnp.float32) * norm_gain[model_index][None, :] * inverse_rms).astype(jnp.bfloat16)
        projected = []
        for kind_index in range(3):
            result = jnp.dot(normed, w_qkv[model_index, kind_index], preferred_element_type=jnp.float32).astype(jnp.bfloat16)
            projected.append(result.reshape(TOKENS, HEADS, HEAD).transpose(1, 0, 2))

        def one_head(operands):
            queries, key_rows, value_rows = operands
            scores = jnp.dot(queries, key_rows.T, preferred_element_type=jnp.float32) / math.sqrt(HEAD)
            scores = jnp.where(allowed, scores, -1e+30)
            row_peak = lax.optimization_barrier(jnp.max(scores, axis=1, keepdims=True))
            weights = jnp.where(allowed, jnp.exp(scores - row_peak), 0.0)
            row_total = lax.optimization_barrier(jnp.sum(weights, axis=1, keepdims=True))
            probabilities = weights.astype(jnp.bfloat16)
            mixed = jnp.dot(probabilities, value_rows, preferred_element_type=jnp.float32)
            return (mixed / row_total).astype(jnp.bfloat16)
        attended = lax.map(one_head, (projected[0], projected[1], projected[2]))
        attended = attended.transpose(1, 0, 2).reshape(TOKENS, HEADS * HEAD)
        out_weight = w_out[model_index]

        def add_group(group_index, running):
            first_col = (group_index * group_width).astype(jnp.int32)
            columns = lax.dynamic_slice_in_dim(attended, first_col, group_width, 1)
            rows_of = lax.dynamic_slice_in_dim(out_weight, first_col, group_width, 0)
            partial_sum = jnp.dot(columns, rows_of, preferred_element_type=jnp.float32).astype(jnp.bfloat16)
            partial_sum = lax.optimization_barrier(partial_sum)
            return running + partial_sum.astype(jnp.float32)
        branch = lax.fori_loop(0, N_CP, add_group, jnp.zeros((TOKENS, D), jnp.float32)).astype(jnp.bfloat16)
        scored = jnp.zeros((NBLK, own_rows, D), jnp.bfloat16).at[block_owner].set(branch.reshape(NBLK, own_rows, D))
        outputs.append(scored.reshape(TOKENS, D))
    return jnp.stack(outputs)
```

```python
import functools
import math

import jax
import jax.numpy as jnp
from jax import lax
from jax.experimental import pallas as pl
from jax.experimental.pallas import tpu as pltpu
from jax.sharding import PartitionSpec as P

HEAD = 128
MESH = pl.DeviceIdType.MESH


def attend_kernel(
    n_sec, n_cp, n_tp,
    rows_ref, gain_ref, owner_ref, lengths_ref, w_ref,
    att_ref,
    xg, xn, wbuf, buf, part, squares, square_rows, inv_cols, keys, values, pos_q, start_q, pos_k,
    w_sem, row_send, row_recv, sq_send, sq_recv, part_send, part_recv, att_send, att_recv,
):
    sec, cp, tp = lax.axis_index("section"), lax.axis_index("cp"), lax.axis_index("tp")
    blocks, own_rows, width = xg.shape
    tokens = blocks * own_rows
    heads = buf.shape[0]
    per_way = heads // 2
    last = n_tp - 1
    pairs = n_cp // 2
    pair, core = cp // 2, cp % 2
    sibling = cp + 1 - 2 * core
    other = 1 - sec
    mine = sec * n_cp + cp

    def weight_copy(head, kind):
        return pltpu.make_async_copy(
            w_ref.at[0, kind, :, pl.ds(pl.multiple_of(head * HEAD, HEAD), HEAD)],
            wbuf.at[head, :, pl.ds(kind * HEAD, HEAD)],
            w_sem.at[head, kind],
        )

    for i in range(per_way):
        for way in range(2):
            for kind in range(3):
                weight_copy(way * per_way + i, kind).start()

    mates = [((pair + k) % pairs) * 2 + core for k in range(1, pairs)]
    barrier = pltpu.get_barrier_semaphore()
    peers = [{"section": other}, {"cp": sibling}]
    peers += [{"cp": m} for m in mates]
    peers += [{"tp": (tp + k) % n_tp} for k in range(1, n_tp)]
    for peer in peers:
        pl.semaphore_signal(barrier, inc=1, device_id=peer, device_id_type=MESH)
    pl.semaphore_wait(barrier, len(peers))

    sent = []

    def send_rows(src, block, peer):
        copy = pltpu.make_async_remote_copy(
            src_ref=src, dst_ref=xg.at[block], send_sem=row_send.at[len(sent)],
            recv_sem=row_recv.at[block], device_id=peer, device_id_type=MESH,
        )
        copy.start()
        sent.append(copy)

    def wait_rows(block):
        pltpu.make_async_remote_copy(
            src_ref=xg.at[block], dst_ref=xg.at[block], send_sem=row_send.at[0],
            recv_sem=row_recv.at[block], device_id={"cp": sibling}, device_id_type=MESH,
        ).wait_recv()

    send_rows(rows_ref, mine, {"section": other})
    for m in mates:
        send_rows(rows_ref, mine, {"cp": m})
    send_rows(rows_ref, mine, {"cp": sibling})
    xg[mine] = rows_ref[...]

    def positions(shape, dim):
        row = lax.broadcasted_iota(jnp.int32, shape, dim)
        pos = jnp.zeros(shape, jnp.int32)
        for b in range(blocks):
            off = row - owner_ref[b] * own_rows
            pos = jnp.where((off >= 0) & (off < own_rows), off + b * own_rows, pos)
        return pos

    pos = positions((tokens, 1), 0)
    pos_q[...] = pos
    start = jnp.zeros((tokens, 1), jnp.int32)
    end = lengths_ref[0]
    for i in range(1, lengths_ref.shape[0] + 1):
        start = jnp.where(pos >= end, end, start)
        if i < lengths_ref.shape[0]:
            end = end + lengths_ref[i]
    start_q[...] = start
    pos_k[...] = positions((1, tokens), 1)

    across = other * n_cp + cp
    wait_rows(across)
    for m in mates:
        send_rows(xg.at[across], across, {"cp": m})
    send_rows(xg.at[across], across, {"cp": sibling})
    for s in (sec, other):
        for k in range(1, pairs):
            block = s * n_cp + ((pair + pairs - k) % pairs) * 2 + core
            wait_rows(block)
            send_rows(xg.at[block], block, {"cp": sibling})
    for s in (sec, other):
        for k in range(pairs):
            wait_rows(s * n_cp + ((pair + k) % pairs) * 2 + 1 - core)

    def scale_block(block, carry):
        x = xg[block].astype(jnp.float32)
        xn[block] = (x * gain_ref[...]).astype(jnp.bfloat16)
        x = x * x
        total = x[:, :HEAD]
        for t in range(1, width // HEAD):
            total += x[:, t * HEAD:(t + 1) * HEAD]
        squares[block] = total
        return carry

    lax.fori_loop(0, blocks, scale_block, 0)
    summed = jnp.sum(squares[...].reshape(tokens, HEAD).T, axis=0, keepdims=True)
    square_rows[tp] = jnp.broadcast_to(summed, (8, tokens))
    square_copies = []
    for k in range(1, n_tp):
        copy = pltpu.make_async_remote_copy(
            src_ref=square_rows.at[tp], dst_ref=square_rows.at[tp], send_sem=sq_send.at[k - 1],
            recv_sem=sq_recv.at[tp], device_id={"tp": (tp + k) % n_tp}, device_id_type=MESH,
        )
        copy.start()
        square_copies.append(copy)

    step_rows = min(tokens, 512)
    query_rows = min(tokens, 256)

    def chain_copy(ref, send_sem, recv_sem, head, to):
        return pltpu.make_async_remote_copy(
            src_ref=ref.at[head], dst_ref=ref.at[head], send_sem=send_sem.at[head],
            recv_sem=recv_sem.at[head], device_id={"tp": to}, device_id_type=MESH,
        )

    def attend(head):
        def normalise(r, carry):
            at = pl.ds(pl.multiple_of(r * query_rows, query_rows), query_rows)
            inv = inv_cols[at, :]
            keys[at, :] = (buf[head, at, HEAD:2 * HEAD].astype(jnp.float32) * inv).astype(jnp.bfloat16)
            values[at, :] = (buf[head, at, 2 * HEAD:].astype(jnp.float32) * inv).astype(jnp.bfloat16)
            return carry

        lax.fori_loop(0, tokens // query_rows, normalise, 0)

        def queries(r, carry):
            at = pl.ds(pl.multiple_of(r * query_rows, query_rows), query_rows)
            q = (buf[head, at, :HEAD].astype(jnp.float32) * inv_cols[at, :]).astype(jnp.bfloat16)
            scores = lax.dot_general(
                q, keys[...], (((1,), (1,)), ((), ())), preferred_element_type=jnp.float32
            ) * (1.0 / math.sqrt(HEAD))
            spot = pos_k[...]
            allowed = (spot <= pos_q[at, :]) & (spot >= start_q[at, :])
            scores = jnp.where(allowed, scores, -1e30)
            peak = jnp.max(scores, axis=1, keepdims=True)
            weights = jnp.where(allowed, jnp.exp(scores - peak), 0.0)
            total = jnp.sum(weights, axis=1, keepdims=True)
            mixed = jnp.dot(
                weights.astype(jnp.bfloat16), values[...], preferred_element_type=jnp.float32
            )
            att_ref[head, at, :] = (mixed / total).astype(jnp.bfloat16)
            return carry

        lax.fori_loop(0, tokens // query_rows, queries, 0)

    def slot(s, carry):
        @pl.when(s == last)
        def _():
            for k in range(1, n_tp):
                src = (tp + k) % n_tp
                pltpu.make_async_remote_copy(
                    src_ref=square_rows.at[src], dst_ref=square_rows.at[src],
                    send_sem=sq_send.at[0], recv_sem=sq_recv.at[src],
                    device_id={"tp": src}, device_id_type=MESH,
                ).wait_recv()
            total = square_rows[0]
            for k in range(1, n_tp):
                total += square_rows[k]
            inv = lax.rsqrt(total[:1] / (width * n_tp) + 1e-05)
            inv_cols[...] = jnp.broadcast_to(inv, (HEAD, tokens)).T

        for way in range(2):
            place = last - tp if way == 0 else tp
            onward = tp - 1 if way == 0 else tp + 1
            back = tp + 1 if way == 0 else tp - 1
            i = s - place
            head = way * per_way + i

            @pl.when((i >= 0) & (i < per_way))
            def _():
                for kind in range(3):
                    weight_copy(head, kind).wait()

                def multiply(r, c):
                    at = pl.ds(pl.multiple_of(r * step_rows, step_rows), step_rows)
                    held = step_rows // own_rows
                    x = xn[pl.ds(r * held, held)].reshape(step_rows, width)
                    part[at, :] = jnp.dot(x, wbuf[head], preferred_element_type=jnp.float32)
                    return c

                lax.fori_loop(0, tokens // step_rows, multiply, 0)

                @pl.when(place == 0)
                def _():
                    buf[head] = part[...].astype(jnp.bfloat16)

                @pl.when(place > 0)
                def _():
                    chain_copy(buf, part_send, part_recv, head, back).wait_recv()
                    buf[head] = (buf[head].astype(jnp.float32) + part[...]).astype(jnp.bfloat16)

                @pl.when(place < last)
                def _():
                    chain_copy(buf, part_send, part_recv, head, onward).start()

        for way in range(2):
            place = last - tp if way == 0 else tp
            onward = tp - 1 if way == 0 else tp + 1
            back = tp + 1 if way == 0 else tp - 1
            i = s - last - (last - place)
            head = way * per_way + i

            @pl.when((i >= 0) & (i < per_way))
            def _():
                @pl.when(place == last)
                def _():
                    attend(head)

                @pl.when(place < last)
                def _():
                    chain_copy(att_ref, att_send, att_recv, head, onward).wait_recv()

                @pl.when(place > 0)
                def _():
                    chain_copy(att_ref, att_send, att_recv, head, back).start()

        return carry

    lax.fori_loop(0, per_way + 2 * last, slot, 0)

    def finish(i, carry):
        for way in range(2):
            place = last - tp if way == 0 else tp
            onward = tp - 1 if way == 0 else tp + 1
            back = tp + 1 if way == 0 else tp - 1
            head = way * per_way + i

            @pl.when(place < last)
            def _():
                chain_copy(buf, part_send, part_recv, head, onward).wait_send()

            @pl.when(place > 0)
            def _():
                chain_copy(att_ref, att_send, att_recv, head, back).wait_send()

        return carry

    lax.fori_loop(0, per_way, finish, 0)
    for copy in sent + square_copies:
        copy.wait_send()


def on_device(rollout_rows, lengths, block_owner, norm_gain, w_qkv, w_out):
    n_tp, n_cp, n_sec = lax.axis_size("tp"), lax.axis_size("cp"), lax.axis_size("section")
    own_rows, width = rollout_rows.shape
    blocks = n_sec * n_cp
    tokens = own_rows * blocks
    columns = w_qkv.shape[3]
    heads = columns // HEAD
    bf16, f32 = jnp.bfloat16, jnp.float32
    sends = 2 + 2 * n_cp
    vmem = pl.BlockSpec(memory_space=pltpu.VMEM)
    smem = pl.BlockSpec(memory_space=pltpu.SMEM)
    dma = pltpu.SemaphoreType.DMA
    attended = pl.pallas_call(
        functools.partial(attend_kernel, n_sec, n_cp, n_tp),
        out_shape=jax.ShapeDtypeStruct((heads, tokens, HEAD), bf16),
        in_specs=[vmem, vmem, smem, smem, pl.BlockSpec(memory_space=pl.ANY)],
        out_specs=vmem,
        scratch_shapes=[
            pltpu.VMEM((blocks, own_rows, width), bf16),
            pltpu.VMEM((blocks, own_rows, width), bf16),
            pltpu.VMEM((heads, width, 3 * HEAD), bf16),
            pltpu.VMEM((heads, tokens, 3 * HEAD), bf16),
            pltpu.VMEM((tokens, 3 * HEAD), f32),
            pltpu.VMEM((blocks, own_rows, HEAD), f32),
            pltpu.VMEM((n_tp, 8, tokens), f32),
            pltpu.VMEM((tokens, HEAD), f32),
            pltpu.VMEM((tokens, HEAD), bf16),
            pltpu.VMEM((tokens, HEAD), bf16),
            pltpu.VMEM((tokens, 1), jnp.int32),
            pltpu.VMEM((tokens, 1), jnp.int32),
            pltpu.VMEM((1, tokens), jnp.int32),
            dma((heads, 3)),
            dma((sends,)),
            dma((blocks,)),
            dma((n_tp,)),
            dma((n_tp,)),
            dma((heads,)),
            dma((heads,)),
            dma((heads,)),
            dma((heads,)),
        ],
        compiler_params=pltpu.CompilerParams(
            collective_id=0, has_side_effects=True, vmem_limit_bytes=60 * 1024 * 1024
        ),
        name="attend",
    )(rollout_rows, norm_gain, block_owner, lengths, w_qkv)
    attended = attended.transpose(1, 0, 2).reshape(n_sec, n_cp, own_rows, columns)
    ordered = attended.transpose(1, 0, 2, 3).reshape(tokens, columns)
    summed = lax.psum_scatter(
        jnp.dot(ordered, w_out[0], preferred_element_type=f32).astype(bf16),
        "cp", scatter_dimension=0, tiled=True,
    )
    branch = summed.reshape(n_sec, own_rows, width)
    return lax.all_to_all(branch, "section", split_axis=0, concat_axis=0, tiled=True)


def solution(mesh):
    return jax.shard_map(
        on_device,
        mesh=mesh,
        in_specs=(
            P(("section", "cp"), "tp"),
            P(),
            P(),
            P("section", "tp"),
            P("section", None, "tp", "cp"),
            P("section", "cp", "tp"),
        ),
        out_specs=P(None, ("section", "cp"), "tp"),
        check_vma=False,
    )
```

```python
import functools
import math

import jax
import jax.numpy as jnp
from jax import lax
from jax.experimental import pallas as pl
from jax.experimental.pallas import tpu as pltpu
from jax.sharding import PartitionSpec as P

HEAD = 128
MESH = pl.DeviceIdType.MESH


def attend_kernel(
    n_sec, n_cp, n_tp,
    rows_ref, gain_ref, owner_ref, lengths_ref, w_ref, w_out_ref,
    out_ref,
    att_ref, w_out_buf, lhs, pair_out, pair_in, sums, mate_in, over,
    xg, xn, wbuf, buf, part, squares, square_rows, inv_cols, keys, values, pos_q, start_q, pos_k,
    w_sem, row_send, row_recv, sq_send, sq_recv, part_send, part_recv, att_send, att_recv,
    out_sem, pair_send, pair_recv, mate_send, mate_recv, home_send, home_recv,
):
    sec, cp, tp = lax.axis_index("section"), lax.axis_index("cp"), lax.axis_index("tp")
    blocks, own_rows, width = xg.shape
    tokens = blocks * own_rows
    heads = buf.shape[0]
    per_way = heads // 2
    last = n_tp - 1
    pairs = n_cp // 2
    pair, core = cp // 2, cp % 2
    sibling = cp + 1 - 2 * core
    other = 1 - sec
    mine = sec * n_cp + cp

    def weight_copy(head, kind):
        return pltpu.make_async_copy(
            w_ref.at[0, kind, :, pl.ds(pl.multiple_of(head * HEAD, HEAD), HEAD)],
            wbuf.at[head, :, pl.ds(kind * HEAD, HEAD)],
            w_sem.at[head, kind],
        )

    for i in range(per_way):
        for way in range(2):
            for kind in range(3):
                weight_copy(way * per_way + i, kind).start()

    out_copy = pltpu.make_async_copy(w_out_ref.at[0], w_out_buf, out_sem)
    out_copy.start()

    mates = [((pair + k) % pairs) * 2 + core for k in range(1, pairs)]
    barrier = pltpu.get_barrier_semaphore()
    peers = [{"section": other}, {"cp": sibling}]
    peers += [{"cp": m} for m in mates]
    peers += [{"tp": (tp + k) % n_tp} for k in range(1, n_tp)]
    for peer in peers:
        pl.semaphore_signal(barrier, inc=1, device_id=peer, device_id_type=MESH)
    pl.semaphore_wait(barrier, len(peers))

    sent = []

    def send_rows(src, block, peer):
        copy = pltpu.make_async_remote_copy(
            src_ref=src, dst_ref=xg.at[block], send_sem=row_send.at[len(sent)],
            recv_sem=row_recv.at[block], device_id=peer, device_id_type=MESH,
        )
        copy.start()
        sent.append(copy)

    def wait_rows(block):
        pltpu.make_async_remote_copy(
            src_ref=xg.at[block], dst_ref=xg.at[block], send_sem=row_send.at[0],
            recv_sem=row_recv.at[block], device_id={"cp": sibling}, device_id_type=MESH,
        ).wait_recv()

    send_rows(rows_ref, mine, {"section": other})
    for m in mates:
        send_rows(rows_ref, mine, {"cp": m})
    send_rows(rows_ref, mine, {"cp": sibling})
    xg[mine] = rows_ref[...]

    def positions(shape, dim):
        row = lax.broadcasted_iota(jnp.int32, shape, dim)
        pos = jnp.zeros(shape, jnp.int32)
        for b in range(blocks):
            off = row - owner_ref[b] * own_rows
            pos = jnp.where((off >= 0) & (off < own_rows), off + b * own_rows, pos)
        return pos

    pos = positions((tokens, 1), 0)
    pos_q[...] = pos
    start = jnp.zeros((tokens, 1), jnp.int32)
    end = lengths_ref[0]
    for i in range(1, lengths_ref.shape[0] + 1):
        start = jnp.where(pos >= end, end, start)
        if i < lengths_ref.shape[0]:
            end = end + lengths_ref[i]
    start_q[...] = start
    pos_k[...] = positions((1, tokens), 1)

    across = other * n_cp + cp
    wait_rows(across)
    for m in mates:
        send_rows(xg.at[across], across, {"cp": m})
    send_rows(xg.at[across], across, {"cp": sibling})
    for s in (sec, other):
        for k in range(1, pairs):
            block = s * n_cp + ((pair + pairs - k) % pairs) * 2 + core
            wait_rows(block)
            send_rows(xg.at[block], block, {"cp": sibling})
    for s in (sec, other):
        for k in range(pairs):
            wait_rows(s * n_cp + ((pair + k) % pairs) * 2 + 1 - core)

    def scale_block(block, carry):
        x = xg[block].astype(jnp.float32)
        xn[block] = (x * gain_ref[...]).astype(jnp.bfloat16)
        x = x * x
        total = x[:, :HEAD]
        for t in range(1, width // HEAD):
            total += x[:, t * HEAD:(t + 1) * HEAD]
        squares[block] = total
        return carry

    lax.fori_loop(0, blocks, scale_block, 0)
    summed = jnp.sum(squares[...].reshape(tokens, HEAD).T, axis=0, keepdims=True)
    square_rows[tp] = jnp.broadcast_to(summed, (8, tokens))
    square_copies = []
    for k in range(1, n_tp):
        copy = pltpu.make_async_remote_copy(
            src_ref=square_rows.at[tp], dst_ref=square_rows.at[tp], send_sem=sq_send.at[k - 1],
            recv_sem=sq_recv.at[tp], device_id={"tp": (tp + k) % n_tp}, device_id_type=MESH,
        )
        copy.start()
        square_copies.append(copy)

    pieces = part_send.shape[1]
    step_rows = tokens // pieces
    query_rows = min(tokens, 256)

    def part_copy(head, piece, to):
        rows = buf.at[head, pl.ds(pl.multiple_of(piece * step_rows, step_rows), step_rows)]
        return pltpu.make_async_remote_copy(
            src_ref=rows, dst_ref=rows, send_sem=part_send.at[head, piece],
            recv_sem=part_recv.at[head, piece], device_id={"tp": to}, device_id_type=MESH,
        )

    def att_copy(head, to):
        return pltpu.make_async_remote_copy(
            src_ref=att_ref.at[head], dst_ref=att_ref.at[head], send_sem=att_send.at[head],
            recv_sem=att_recv.at[head], device_id={"tp": to}, device_id_type=MESH,
        )

    def attend(head):
        def normalise(r, carry):
            at = pl.ds(pl.multiple_of(r * query_rows, query_rows), query_rows)
            inv = inv_cols[at, :]
            keys[at, :] = (buf[head, at, HEAD:2 * HEAD].astype(jnp.float32) * inv).astype(jnp.bfloat16)
            values[at, :] = (buf[head, at, 2 * HEAD:].astype(jnp.float32) * inv).astype(jnp.bfloat16)
            return carry

        lax.fori_loop(0, tokens // query_rows, normalise, 0)

        def queries(r, carry):
            at = pl.ds(pl.multiple_of(r * query_rows, query_rows), query_rows)
            q = (buf[head, at, :HEAD].astype(jnp.float32) * inv_cols[at, :]).astype(jnp.bfloat16)
            scores = lax.dot_general(
                q, keys[...], (((1,), (1,)), ((), ())), preferred_element_type=jnp.float32
            ) * (1.0 / math.sqrt(HEAD))
            spot = pos_k[...]
            allowed = (spot <= pos_q[at, :]) & (spot >= start_q[at, :])
            scores = jnp.where(allowed, scores, -1e30)
            peak = jnp.max(scores, axis=1, keepdims=True)
            weights = jnp.where(allowed, jnp.exp(scores - peak), 0.0)
            total = jnp.sum(weights, axis=1, keepdims=True)
            mixed = jnp.dot(
                weights.astype(jnp.bfloat16), values[...], preferred_element_type=jnp.float32
            )
            held = query_rows // own_rows
            att_ref[head, pl.ds(r * held, held)] = (
                (mixed / total).astype(jnp.bfloat16).reshape(held, own_rows, HEAD)
            )
            return carry

        lax.fori_loop(0, tokens // query_rows, queries, 0)

    def slot(s, carry):
        @pl.when(s == last)
        def _():
            for k in range(1, n_tp):
                src = (tp + k) % n_tp
                pltpu.make_async_remote_copy(
                    src_ref=square_rows.at[src], dst_ref=square_rows.at[src],
                    send_sem=sq_send.at[0], recv_sem=sq_recv.at[src],
                    device_id={"tp": src}, device_id_type=MESH,
                ).wait_recv()
            total = square_rows[0]
            for k in range(1, n_tp):
                total += square_rows[k]
            inv = lax.rsqrt(total[:1] / (width * n_tp) + 1e-05)
            inv_cols[...] = jnp.broadcast_to(inv, (HEAD, tokens)).T

        def partial_sums(o, c):
            way = (first + o) % 2
            place = way * tp + (1 - way) * (last - tp)
            onward, back = tp + 2 * way - 1, tp - 2 * way + 1
            i = s - place
            head = way * per_way + i

            @pl.when((i >= 0) & (i < per_way))
            def _():
                for kind in range(3):
                    weight_copy(head, kind).wait()

                def multiply(r, c):
                    at = pl.ds(pl.multiple_of(r * step_rows, step_rows), step_rows)
                    held = step_rows // own_rows
                    x = xn[pl.ds(r * held, held)].reshape(step_rows, width)
                    part[...] = jnp.dot(x, wbuf[head], preferred_element_type=jnp.float32)

                    @pl.when(place == 0)
                    def _():
                        buf[head, at, :] = part[...].astype(jnp.bfloat16)

                    @pl.when(place > 0)
                    def _():
                        part_copy(head, r, back).wait_recv()
                        held_sum = buf[head, at, :].astype(jnp.float32)
                        buf[head, at, :] = (held_sum + part[...]).astype(jnp.bfloat16)

                    @pl.when(place < last)
                    def _():
                        part_copy(head, r, onward).start()

                    return c

                lax.fori_loop(0, pieces, multiply, 0)

            return c

        lax.fori_loop(0, 2, partial_sums, 0)

        def attended_rows(o, c):
            way = (first + 1 + o) % 2
            place = way * tp + (1 - way) * (last - tp)
            onward, back = tp + 2 * way - 1, tp - 2 * way + 1
            i = s - last - (last - place)
            head = way * per_way + i

            @pl.when((i >= 0) & (i < per_way))
            def _():
                @pl.when(place == last)
                def _():
                    attend(head)

                @pl.when(place < last)
                def _():
                    att_copy(head, onward).wait_recv()

                @pl.when(place > 0)
                def _():
                    att_copy(head, back).start()

            return c

        lax.fori_loop(0, 2, attended_rows, 0)
        return carry

    first = 1 - (2 * tp) // n_tp
    lax.fori_loop(0, per_way + 2 * last, slot, 0)

    out_copy.wait()
    columns = lhs.shape[1]
    tile = min(width, 512)

    def project(section, to_core, target, arrived):
        for k in range(pairs):
            block = section * n_cp + 2 * k + to_core
            for h in range(heads):
                lhs[k * own_rows:(k + 1) * own_rows, h * HEAD:(h + 1) * HEAD] = att_ref[h, block]

        def one_tile(t, c):
            at = pl.ds(pl.multiple_of(t * tile, tile), tile)
            product = jnp.dot(
                lhs[...], w_out_buf[:, at], preferred_element_type=jnp.float32
            ).reshape(pairs, own_rows, tile)
            if arrived is not None:
                product += arrived[section, :, :, at].astype(jnp.float32)
            target[section, :, :, at] = product.astype(jnp.bfloat16)
            return c

        lax.fori_loop(0, width // tile, one_tile, 0)

    def pair_copy(section):
        return pltpu.make_async_remote_copy(
            src_ref=pair_out.at[section], dst_ref=pair_in.at[section],
            send_sem=pair_send.at[section], recv_sem=pair_recv.at[section],
            device_id={"cp": sibling}, device_id_type=MESH,
        )

    def mate_copy(section, k):
        to = (pair + k) % pairs
        return pltpu.make_async_remote_copy(
            src_ref=sums.at[section, to], dst_ref=mate_in.at[section, pair],
            send_sem=mate_send.at[section, to], recv_sem=mate_recv.at[section, pair],
            device_id={"cp": 2 * to + core}, device_id_type=MESH,
        )

    def wait_mate(section, k):
        src = (pair + pairs - k) % pairs
        pltpu.make_async_remote_copy(
            src_ref=mate_in.at[section, src], dst_ref=mate_in.at[section, src],
            send_sem=mate_send.at[section, src], recv_sem=mate_recv.at[section, src],
            device_id={"cp": 2 * src + core}, device_id_type=MESH,
        ).wait_recv()

    def total_of(section):
        total = sums[section, pair].astype(jnp.float32)
        for k in range(1, pairs):
            wait_mate(section, k)
            total += mate_in[section, (pair + pairs - k) % pairs].astype(jnp.float32)
        return total.astype(jnp.bfloat16)

    for section in (other, sec):
        project(section, 1 - core, pair_out, None)
        pair_copy(section).start()
        pair_copy(section).wait_recv()
        project(section, core, sums, pair_in)
        for k in range(1, pairs):
            mate_copy(section, k).start()

    over[...] = total_of(other)
    home = pltpu.make_async_remote_copy(
        src_ref=over, dst_ref=out_ref.at[sec], send_sem=home_send, recv_sem=home_recv,
        device_id={"section": other}, device_id_type=MESH,
    )
    home.start()
    out_ref[sec] = total_of(sec)
    home.wait()
    for section in (other, sec):
        pair_copy(section).wait_send()
        for k in range(1, pairs):
            mate_copy(section, k).wait_send()

    def finish(i, carry):
        for way in range(2):
            place = last - tp if way == 0 else tp
            onward = tp - 1 if way == 0 else tp + 1
            back = tp + 1 if way == 0 else tp - 1
            head = way * per_way + i

            @pl.when(place < last)
            def _():
                for piece in range(pieces):
                    part_copy(head, piece, onward).wait_send()

            @pl.when(place > 0)
            def _():
                att_copy(head, back).wait_send()

        return carry

    lax.fori_loop(0, per_way, finish, 0)
    for copy in sent + square_copies:
        copy.wait_send()


def on_device(rollout_rows, lengths, block_owner, norm_gain, w_qkv, w_out):
    n_tp, n_cp, n_sec = lax.axis_size("tp"), lax.axis_size("cp"), lax.axis_size("section")
    own_rows, width = rollout_rows.shape
    blocks = n_sec * n_cp
    tokens = own_rows * blocks
    columns = w_qkv.shape[3]
    heads = columns // HEAD
    bf16, f32 = jnp.bfloat16, jnp.float32
    sends = 2 + 2 * n_cp
    vmem = pl.BlockSpec(memory_space=pltpu.VMEM)
    smem = pl.BlockSpec(memory_space=pltpu.SMEM)
    dma = pltpu.SemaphoreType.DMA
    pairs = n_cp // 2
    pieces = max(2, tokens // 512)
    exchange = pltpu.VMEM((n_sec, pairs, own_rows, width), bf16)
    return pl.pallas_call(
        functools.partial(attend_kernel, n_sec, n_cp, n_tp),
        out_shape=jax.ShapeDtypeStruct((n_sec, own_rows, width), bf16),
        in_specs=[vmem, vmem, smem, smem] + [pl.BlockSpec(memory_space=pl.ANY)] * 2,
        out_specs=vmem,
        scratch_shapes=[
            pltpu.VMEM((heads, blocks, own_rows, HEAD), bf16),
            pltpu.VMEM((columns, width), bf16),
            pltpu.VMEM((pairs * own_rows, columns), bf16),
            exchange,
            exchange,
            exchange,
            exchange,
            pltpu.VMEM((own_rows, width), bf16),
            pltpu.VMEM((blocks, own_rows, width), bf16),
            pltpu.VMEM((blocks, own_rows, width), bf16),
            pltpu.VMEM((heads, width, 3 * HEAD), bf16),
            pltpu.VMEM((heads, tokens, 3 * HEAD), bf16),
            pltpu.VMEM((tokens // pieces, 3 * HEAD), f32),
            pltpu.VMEM((blocks, own_rows, HEAD), f32),
            pltpu.VMEM((n_tp, 8, tokens), f32),
            pltpu.VMEM((tokens, HEAD), f32),
            pltpu.VMEM((tokens, HEAD), bf16),
            pltpu.VMEM((tokens, HEAD), bf16),
            pltpu.VMEM((tokens, 1), jnp.int32),
            pltpu.VMEM((tokens, 1), jnp.int32),
            pltpu.VMEM((1, tokens), jnp.int32),
            dma((heads, 3)),
            dma((sends,)),
            dma((blocks,)),
            dma((n_tp,)),
            dma((n_tp,)),
            dma((heads, pieces)),
            dma((heads, pieces)),
            dma((heads,)),
            dma((heads,)),
            dma,
            dma((n_sec,)),
            dma((n_sec,)),
            dma((n_sec, pairs)),
            dma((n_sec, pairs)),
            dma,
            dma,
        ],
        compiler_params=pltpu.CompilerParams(
            collective_id=0, has_side_effects=True, vmem_limit_bytes=62 * 1024 * 1024
        ),
        name="attend",
    )(rollout_rows, norm_gain, block_owner, lengths, w_qkv, w_out)


def solution(mesh):
    return jax.shard_map(
        on_device,
        mesh=mesh,
        in_specs=(
            P(("section", "cp"), "tp"),
            P(),
            P(),
            P("section", "tp"),
            P("section", None, "tp", "cp"),
            P("section", "cp", "tp"),
        ),
        out_specs=P(None, ("section", "cp"), "tp"),
        check_vma=False,
    )
```

```python
import functools
import math

import jax
import jax.numpy as jnp
from jax import lax
from jax.experimental import pallas as pl
from jax.experimental.pallas import tpu as pltpu
from jax.sharding import PartitionSpec as P

HEAD = 128
MESH = pl.DeviceIdType.MESH


def attend_kernel(
    n_sec, n_cp, n_tp,
    rows_ref, gain_ref, owner_ref, lengths_ref, w_ref, w_out_ref,
    out_ref,
    att_ref, w_out_buf, lhs, pair_out, pair_in, sums, mate_in, over,
    xg, xn, wbuf, buf, part, squares, square_rows, inv_cols, keys, values, pos_q, start_q, pos_k,
    w_sem, row_send, row_recv, sq_send, sq_recv, part_send, part_recv, att_send, att_recv,
    out_sem, pair_send, pair_recv, mate_send, mate_recv, home_send, home_recv,
):
    sec, cp, tp = lax.axis_index("section"), lax.axis_index("cp"), lax.axis_index("tp")
    blocks, own_rows, width = xg.shape
    tokens = blocks * own_rows
    heads = buf.shape[0]
    per_way = heads // 2
    last = n_tp - 1
    pairs = n_cp // 2
    pair, core = cp // 2, cp % 2
    sibling = cp + 1 - 2 * core
    other = 1 - sec
    mine = sec * n_cp + cp

    def weight_copy(head, kind):
        return pltpu.make_async_copy(
            w_ref.at[0, kind, :, pl.ds(pl.multiple_of(head * HEAD, HEAD), HEAD)],
            wbuf.at[head, :, pl.ds(kind * HEAD, HEAD)],
            w_sem.at[head, kind],
        )

    for i in range(per_way):
        for way in range(2):
            for kind in range(3):
                weight_copy(way * per_way + i, kind).start()

    out_copy = pltpu.make_async_copy(w_out_ref.at[0], w_out_buf, out_sem)
    out_copy.start()

    mates = [((pair + k) % pairs) * 2 + core for k in range(1, pairs)]
    barrier = pltpu.get_barrier_semaphore()
    peers = [{"section": other}, {"cp": sibling}]
    peers += [{"cp": m} for m in mates]
    peers += [{"tp": (tp + k) % n_tp} for k in range(1, n_tp)]
    for peer in peers:
        pl.semaphore_signal(barrier, inc=1, device_id=peer, device_id_type=MESH)
    pl.semaphore_wait(barrier, len(peers))

    sent = []

    def send_rows(src, block, peer):
        copy = pltpu.make_async_remote_copy(
            src_ref=src, dst_ref=xg.at[block], send_sem=row_send.at[len(sent)],
            recv_sem=row_recv.at[block], device_id=peer, device_id_type=MESH,
        )
        copy.start()
        sent.append(copy)

    def wait_rows(block):
        pltpu.make_async_remote_copy(
            src_ref=xg.at[block], dst_ref=xg.at[block], send_sem=row_send.at[0],
            recv_sem=row_recv.at[block], device_id={"cp": sibling}, device_id_type=MESH,
        ).wait_recv()

    send_rows(rows_ref, mine, {"section": other})
    for m in mates:
        send_rows(rows_ref, mine, {"cp": m})
    send_rows(rows_ref, mine, {"cp": sibling})
    xg[mine] = rows_ref[...]

    def positions(shape, dim):
        row = lax.broadcasted_iota(jnp.int32, shape, dim)
        pos = jnp.zeros(shape, jnp.int32)
        for b in range(blocks):
            off = row - owner_ref[b] * own_rows
            pos = jnp.where((off >= 0) & (off < own_rows), off + b * own_rows, pos)
        return pos

    pos = positions((tokens, 1), 0)
    pos_q[...] = pos
    start = jnp.zeros((tokens, 1), jnp.int32)
    end = lengths_ref[0]
    for i in range(1, lengths_ref.shape[0] + 1):
        start = jnp.where(pos >= end, end, start)
        if i < lengths_ref.shape[0]:
            end = end + lengths_ref[i]
    start_q[...] = start
    pos_k[...] = positions((1, tokens), 1)

    pieces = n_sec * pairs
    step_rows = 2 * own_rows
    query_rows = min(tokens, 256)
    att_pieces = tokens // query_rows
    group = min(4, per_way)
    lead = group * pieces
    first = 1 - (2 * tp) // n_tp

    def piece_block(q):
        section = sec + (q % 2) * (other - sec)
        return section * n_cp + 2 * ((pair + pairs - q // 2) % pairs)

    def part_copy(head, q, to):
        rows = buf.at[head, pl.ds(pl.multiple_of(piece_block(q) * own_rows, step_rows), step_rows)]
        return pltpu.make_async_remote_copy(
            src_ref=rows, dst_ref=rows, send_sem=part_send.at[head, q],
            recv_sem=part_recv.at[head, q], device_id={"tp": to}, device_id_type=MESH,
        )

    def att_copy(head, r, to):
        held = query_rows // own_rows
        rows = att_ref.at[head, pl.ds(r * held, held)]
        return pltpu.make_async_remote_copy(
            src_ref=rows, dst_ref=rows, send_sem=att_send.at[head, r],
            recv_sem=att_recv.at[head, r], device_id={"tp": to}, device_id_type=MESH,
        )

    def multiply(head, q):
        block = piece_block(q)
        x = xn[pl.ds(block, 2)].reshape(step_rows, width)
        part[...] = jnp.dot(x, wbuf[head], preferred_element_type=jnp.float32)
        return pl.ds(pl.multiple_of(block * own_rows, step_rows), step_rows)

    def scale_block(block):
        x = xg[block].astype(jnp.float32)
        xn[block] = (x * gain_ref[...]).astype(jnp.bfloat16)
        x = x * x
        total = x[:, :HEAD]
        for t in range(1, width // HEAD):
            total += x[:, t * HEAD:(t + 1) * HEAD]
        squares[block] = total

    def begin(q):
        def scale(k, c):
            scale_block(piece_block(q) + k)
            return c

        lax.fori_loop(0, 2, scale, 0)

        @pl.when((tp == 0) | (tp == last))
        def _():
            def one_head(j, c):
                head = first * per_way + j
                if q == 0:
                    for kind in range(3):
                        weight_copy(head, kind).wait()
                at = multiply(head, q)
                buf[head, at, :] = part[...].astype(jnp.bfloat16)
                part_copy(head, q, tp + 2 * first - 1).start()
                return c

            lax.fori_loop(0, group, one_head, 0)

    across = other * n_cp + cp
    wait_rows(mine + 1 - 2 * core)
    begin(0)
    wait_rows(across)
    for m in mates:
        send_rows(xg.at[across], across, {"cp": m})
    send_rows(xg.at[across], across, {"cp": sibling})
    for k in range(1, pairs):
        block = sec * n_cp + ((pair + pairs - k) % pairs) * 2 + core
        wait_rows(block)
        send_rows(xg.at[block], block, {"cp": sibling})
    wait_rows(across + 1 - 2 * core)
    begin(1)
    for k in range(1, pairs):
        block = other * n_cp + ((pair + pairs - k) % pairs) * 2 + core
        wait_rows(block)
        send_rows(xg.at[block], block, {"cp": sibling})
    for k in range(1, pairs):
        for i, side in enumerate((sec, other)):
            wait_rows(side * n_cp + ((pair + pairs - k) % pairs) * 2 + 1 - core)
            begin(2 * k + i)

    summed = jnp.sum(squares[...].reshape(tokens, HEAD).T, axis=0, keepdims=True)
    square_rows[tp] = jnp.broadcast_to(summed, (8, tokens))
    square_copies = []
    for k in range(1, n_tp):
        copy = pltpu.make_async_remote_copy(
            src_ref=square_rows.at[tp], dst_ref=square_rows.at[tp], send_sem=sq_send.at[k - 1],
            recv_sem=sq_recv.at[tp], device_id={"tp": (tp + k) % n_tp}, device_id_type=MESH,
        )
        copy.start()
        square_copies.append(copy)

    def attend(head, back):
        def normalise(r, carry):
            at = pl.ds(pl.multiple_of(r * query_rows, query_rows), query_rows)
            inv = inv_cols[at, :]
            keys[at, :] = (buf[head, at, HEAD:2 * HEAD].astype(jnp.float32) * inv).astype(jnp.bfloat16)
            values[at, :] = (buf[head, at, 2 * HEAD:].astype(jnp.float32) * inv).astype(jnp.bfloat16)
            return carry

        lax.fori_loop(0, tokens // query_rows, normalise, 0)

        def queries(r, carry):
            at = pl.ds(pl.multiple_of(r * query_rows, query_rows), query_rows)
            q = (buf[head, at, :HEAD].astype(jnp.float32) * inv_cols[at, :]).astype(jnp.bfloat16)
            scores = lax.dot_general(
                q, keys[...], (((1,), (1,)), ((), ())), preferred_element_type=jnp.float32
            ) * (1.0 / math.sqrt(HEAD))
            spot = pos_k[...]
            allowed = (spot <= pos_q[at, :]) & (spot >= start_q[at, :])
            scores = jnp.where(allowed, scores, -1e30)
            peak = jnp.max(scores, axis=1, keepdims=True)
            weights = jnp.where(allowed, jnp.exp(scores - peak), 0.0)
            total = jnp.sum(weights, axis=1, keepdims=True)
            mixed = jnp.dot(
                weights.astype(jnp.bfloat16), values[...], preferred_element_type=jnp.float32
            )
            held = query_rows // own_rows
            att_ref[head, pl.ds(r * held, held)] = (
                (mixed / total).astype(jnp.bfloat16).reshape(held, own_rows, HEAD)
            )
            att_copy(head, r, back).start()
            return carry

        lax.fori_loop(0, tokens // query_rows, queries, 0)

    def slot(s, carry):
        @pl.when(s == 2)
        def _():
            for k in range(1, n_tp):
                src = (tp + k) % n_tp
                pltpu.make_async_remote_copy(
                    src_ref=square_rows.at[src], dst_ref=square_rows.at[src],
                    send_sem=sq_send.at[0], recv_sem=sq_recv.at[src],
                    device_id={"tp": src}, device_id_type=MESH,
                ).wait_recv()
            total = square_rows[0]
            for k in range(1, n_tp):
                total += square_rows[k]
            inv = lax.rsqrt(total[:1] / (width * n_tp) + 1e-05)
            inv_cols[...] = jnp.broadcast_to(inv, (HEAD, tokens)).T

        def partial_sums(o, c):
            way = (first + o) % 2
            place = way * tp + (1 - way) * (last - tp)
            onward, back = tp + 2 * way - 1, tp - 2 * way + 1

            @pl.when(place == 0)
            def _():
                i = s + lead

                @pl.when(i < steps)
                def _():
                    head, q = decode(i)
                    head = way * per_way + head

                    @pl.when(q == 0)
                    def _():
                        for kind in range(3):
                            weight_copy(head, kind).wait()

                    at = multiply(head, q)
                    buf[head, at, :] = part[...].astype(jnp.bfloat16)
                    part_copy(head, q, onward).start()

            @pl.when(place > 0)
            def _():
                i = s - (place - 1) * hop

                @pl.when((i >= 0) & (i < steps))
                def _():
                    head, q = decode(i)
                    head = way * per_way + head

                    @pl.when(q == 0)
                    def _():
                        for kind in range(3):
                            weight_copy(head, kind).wait()

                    at = multiply(head, q)
                    part_copy(head, q, back).wait_recv()
                    held_sum = buf[head, at, :].astype(jnp.float32)
                    buf[head, at, :] = (held_sum + part[...]).astype(jnp.bfloat16)

                    @pl.when(place < last)
                    def _():
                        part_copy(head, q, onward).start()

            return c

        lax.fori_loop(0, 2, partial_sums, 0)

        def attended_rows(o, c):
            way = (first + 1 + o) % 2
            place = way * tp + (1 - way) * (last - tp)
            onward, back = tp + 2 * way - 1, tp - 2 * way + 1
            i = s - (last - 1) * hop - (last - place) * back_hop

            @pl.when((i >= 0) & (i < steps))
            def _():
                head, q = decode(i)
                head = way * per_way + head

                @pl.when(q == pieces - 1)
                def _():
                    @pl.when(place == last)
                    def _():
                        attend(head, back)

                    @pl.when(place < last)
                    def _():
                        def pass_on(r, d):
                            att_copy(head, r, onward).wait_recv()

                            @pl.when(place > 0)
                            def _():
                                att_copy(head, r, back).start()

                            return d

                        lax.fori_loop(0, att_pieces, pass_on, 0)

            return c

        lax.fori_loop(0, 2, attended_rows, 0)
        return carry

    steps = per_way * pieces
    hop, back_hop = 3, 3

    def decode(i):
        early = i < lead
        return (
            jnp.where(early, i % group, i // pieces),
            jnp.where(early, i // group, i % pieces),
        )

    lax.fori_loop(0, steps + (last - 1) * hop + last * back_hop, slot, 0)

    out_copy.wait()
    columns = lhs.shape[1]
    tile = min(width, 512)

    def project(section, to_core, target, arrived):
        for k in range(pairs):
            block = section * n_cp + 2 * k + to_core
            for h in range(heads):
                lhs[k * own_rows:(k + 1) * own_rows, h * HEAD:(h + 1) * HEAD] = att_ref[h, block]

        def one_tile(t, c):
            at = pl.ds(pl.multiple_of(t * tile, tile), tile)
            product = jnp.dot(
                lhs[...], w_out_buf[:, at], preferred_element_type=jnp.float32
            ).reshape(pairs, own_rows, tile)
            if arrived is not None:
                product += arrived[section, :, :, at].astype(jnp.float32)
            target[section, :, :, at] = product.astype(jnp.bfloat16)
            return c

        lax.fori_loop(0, width // tile, one_tile, 0)

    def pair_copy(section):
        return pltpu.make_async_remote_copy(
            src_ref=pair_out.at[section], dst_ref=pair_in.at[section],
            send_sem=pair_send.at[section], recv_sem=pair_recv.at[section],
            device_id={"cp": sibling}, device_id_type=MESH,
        )

    def mate_copy(section, k):
        to = (pair + k) % pairs
        return pltpu.make_async_remote_copy(
            src_ref=sums.at[section, to], dst_ref=mate_in.at[section, pair],
            send_sem=mate_send.at[section, to], recv_sem=mate_recv.at[section, pair],
            device_id={"cp": 2 * to + core}, device_id_type=MESH,
        )

    def wait_mate(section, k):
        src = (pair + pairs - k) % pairs
        pltpu.make_async_remote_copy(
            src_ref=mate_in.at[section, src], dst_ref=mate_in.at[section, src],
            send_sem=mate_send.at[section, src], recv_sem=mate_recv.at[section, src],
            device_id={"cp": 2 * src + core}, device_id_type=MESH,
        ).wait_recv()

    def total_of(section):
        total = sums[section, pair].astype(jnp.float32)
        for k in range(1, pairs):
            wait_mate(section, k)
            total += mate_in[section, (pair + pairs - k) % pairs].astype(jnp.float32)
        return total.astype(jnp.bfloat16)

    for section in (other, sec):
        project(section, 1 - core, pair_out, None)
        pair_copy(section).start()
        pair_copy(section).wait_recv()
        project(section, core, sums, pair_in)
        for k in range(1, pairs):
            mate_copy(section, k).start()

    over[...] = total_of(other)
    home = pltpu.make_async_remote_copy(
        src_ref=over, dst_ref=out_ref.at[sec], send_sem=home_send, recv_sem=home_recv,
        device_id={"section": other}, device_id_type=MESH,
    )
    home.start()
    out_ref[sec] = total_of(sec)
    home.wait()
    for section in (other, sec):
        pair_copy(section).wait_send()
        for k in range(1, pairs):
            mate_copy(section, k).wait_send()

    def finish(i, carry):
        for way in range(2):
            place = last - tp if way == 0 else tp
            onward = tp - 1 if way == 0 else tp + 1
            back = tp + 1 if way == 0 else tp - 1
            head = way * per_way + i

            @pl.when(place < last)
            def _():
                for piece in range(pieces):
                    part_copy(head, piece, onward).wait_send()

            @pl.when(place > 0)
            def _():
                for r in range(att_pieces):
                    att_copy(head, r, back).wait_send()

        return carry

    lax.fori_loop(0, per_way, finish, 0)
    for copy in sent + square_copies:
        copy.wait_send()


def on_device(rollout_rows, lengths, block_owner, norm_gain, w_qkv, w_out):
    n_tp, n_cp, n_sec = lax.axis_size("tp"), lax.axis_size("cp"), lax.axis_size("section")
    own_rows, width = rollout_rows.shape
    blocks = n_sec * n_cp
    tokens = own_rows * blocks
    columns = w_qkv.shape[3]
    heads = columns // HEAD
    bf16, f32 = jnp.bfloat16, jnp.float32
    sends = 2 + 2 * n_cp
    vmem = pl.BlockSpec(memory_space=pltpu.VMEM)
    smem = pl.BlockSpec(memory_space=pltpu.SMEM)
    dma = pltpu.SemaphoreType.DMA
    pairs = n_cp // 2
    pieces = n_sec * pairs
    att_pieces = tokens // min(tokens, 256)
    exchange = pltpu.VMEM((n_sec, pairs, own_rows, width), bf16)
    return pl.pallas_call(
        functools.partial(attend_kernel, n_sec, n_cp, n_tp),
        out_shape=jax.ShapeDtypeStruct((n_sec, own_rows, width), bf16),
        in_specs=[vmem, vmem, smem, smem] + [pl.BlockSpec(memory_space=pl.ANY)] * 2,
        out_specs=vmem,
        scratch_shapes=[
            pltpu.VMEM((heads, blocks, own_rows, HEAD), bf16),
            pltpu.VMEM((columns, width), bf16),
            pltpu.VMEM((pairs * own_rows, columns), bf16),
            exchange,
            exchange,
            exchange,
            exchange,
            pltpu.VMEM((own_rows, width), bf16),
            pltpu.VMEM((blocks, own_rows, width), bf16),
            pltpu.VMEM((blocks, own_rows, width), bf16),
            pltpu.VMEM((heads, width, 3 * HEAD), bf16),
            pltpu.VMEM((heads, tokens, 3 * HEAD), bf16),
            pltpu.VMEM((2 * own_rows, 3 * HEAD), f32),
            pltpu.VMEM((blocks, own_rows, HEAD), f32),
            pltpu.VMEM((n_tp, 8, tokens), f32),
            pltpu.VMEM((tokens, HEAD), f32),
            pltpu.VMEM((tokens, HEAD), bf16),
            pltpu.VMEM((tokens, HEAD), bf16),
            pltpu.VMEM((tokens, 1), jnp.int32),
            pltpu.VMEM((tokens, 1), jnp.int32),
            pltpu.VMEM((1, tokens), jnp.int32),
            dma((heads, 3)),
            dma((sends,)),
            dma((blocks,)),
            dma((n_tp,)),
            dma((n_tp,)),
            dma((heads, pieces)),
            dma((heads, pieces)),
            dma((heads, att_pieces)),
            dma((heads, att_pieces)),
            dma,
            dma((n_sec,)),
            dma((n_sec,)),
            dma((n_sec, pairs)),
            dma((n_sec, pairs)),
            dma,
            dma,
        ],
        compiler_params=pltpu.CompilerParams(
            collective_id=0, has_side_effects=True, vmem_limit_bytes=62 * 1024 * 1024
        ),
        name="attend",
    )(rollout_rows, norm_gain, block_owner, lengths, w_qkv, w_out)


def solution(mesh):
    return jax.shard_map(
        on_device,
        mesh=mesh,
        in_specs=(
            P(("section", "cp"), "tp"),
            P(),
            P(),
            P("section", "tp"),
            P("section", None, "tp", "cp"),
            P("section", "cp", "tp"),
        ),
        out_specs=P(None, ("section", "cp"), "tp"),
        check_vma=False,
    )
```

```python
import functools
import math

import jax
import jax.numpy as jnp
from jax import lax
from jax.experimental import pallas as pl
from jax.experimental.pallas import tpu as pltpu
from jax.sharding import PartitionSpec as P

HEAD = 128
MESH = pl.DeviceIdType.MESH


def attend_kernel(
    n_sec, n_cp, n_tp,
    rows_ref, gain_ref, owner_ref, lengths_ref, w_ref, w_out_ref,
    out_ref,
    att_ref, w_out_buf, lhs, pair_out, pair_in, sums, mate_in, over,
    xg, xn, wbuf, buf, part, squares, square_rows, inv_cols, keys, values, pos_q, start_q, pos_k,
    w_sem, row_send, row_recv, sq_send, sq_recv, part_send, part_recv, att_send, att_recv,
    out_sem, pair_send, pair_recv, mate_send, mate_recv, home_send, home_recv,
):
    sec, cp, tp = lax.axis_index("section"), lax.axis_index("cp"), lax.axis_index("tp")
    blocks, own_rows, width = xg.shape
    tokens = blocks * own_rows
    heads = buf.shape[0]
    per_way = heads // 2
    last = n_tp - 1
    pairs = n_cp // 2
    pair, core = cp // 2, cp % 2
    sibling = cp + 1 - 2 * core
    other = 1 - sec
    mine = sec * n_cp + cp

    def weight_copy(head, kind):
        return pltpu.make_async_copy(
            w_ref.at[0, kind, :, pl.ds(pl.multiple_of(head * HEAD, HEAD), HEAD)],
            wbuf.at[head, :, pl.ds(kind * HEAD, HEAD)],
            w_sem.at[head, kind],
        )

    for i in range(per_way):
        for way in range(2):
            for kind in range(3):
                weight_copy(way * per_way + i, kind).start()

    out_copy = pltpu.make_async_copy(w_out_ref.at[0], w_out_buf, out_sem)
    out_copy.start()

    mates = [((pair + k) % pairs) * 2 + core for k in range(1, pairs)]
    barrier = pltpu.get_barrier_semaphore()
    peers = [{"section": other}, {"cp": sibling}]
    peers += [{"cp": m} for m in mates]
    peers += [{"tp": (tp + k) % n_tp} for k in range(1, n_tp)]
    for peer in peers:
        pl.semaphore_signal(barrier, inc=1, device_id=peer, device_id_type=MESH)
    pl.semaphore_wait(barrier, len(peers))

    sent = []

    def send_rows(src, block, peer):
        copy = pltpu.make_async_remote_copy(
            src_ref=src, dst_ref=xg.at[block], send_sem=row_send.at[len(sent)],
            recv_sem=row_recv.at[block], device_id=peer, device_id_type=MESH,
        )
        copy.start()
        sent.append(copy)

    def wait_rows(block):
        pltpu.make_async_remote_copy(
            src_ref=xg.at[block], dst_ref=xg.at[block], send_sem=row_send.at[0],
            recv_sem=row_recv.at[block], device_id={"cp": sibling}, device_id_type=MESH,
        ).wait_recv()

    send_rows(rows_ref, mine, {"section": other})
    for m in mates:
        send_rows(rows_ref, mine, {"cp": m})
    send_rows(rows_ref, mine, {"cp": sibling})
    xg[mine] = rows_ref[...]

    def positions(shape, dim):
        row = lax.broadcasted_iota(jnp.int32, shape, dim)
        pos = jnp.zeros(shape, jnp.int32)
        for b in range(blocks):
            off = row - owner_ref[b] * own_rows
            pos = jnp.where((off >= 0) & (off < own_rows), off + b * own_rows, pos)
        return pos

    pos = positions((tokens, 1), 0)
    pos_q[...] = pos
    start = jnp.zeros((tokens, 1), jnp.int32)
    end = lengths_ref[0]
    for i in range(1, lengths_ref.shape[0] + 1):
        start = jnp.where(pos >= end, end, start)
        if i < lengths_ref.shape[0]:
            end = end + lengths_ref[i]
    start_q[...] = start
    pos_k[...] = positions((1, tokens), 1)

    pieces = n_sec * pairs
    step_rows = 2 * own_rows
    query_rows = min(tokens, 256)
    att_pieces = tokens // query_rows
    group = min(2, per_way)
    lead = group * pieces
    first = 1 - (2 * tp) // n_tp

    def piece_block(q):
        section = sec + (q % 2) * (other - sec)
        return section * n_cp + 2 * ((pair + pairs - q // 2) % pairs)

    def part_copy(head, q, to):
        rows = buf.at[head, pl.ds(pl.multiple_of(piece_block(q) * own_rows, step_rows), step_rows)]
        return pltpu.make_async_remote_copy(
            src_ref=rows, dst_ref=rows, send_sem=part_send.at[head, q],
            recv_sem=part_recv.at[head, q], device_id={"tp": to}, device_id_type=MESH,
        )

    def att_copy(head, r, to):
        held = query_rows // own_rows
        rows = att_ref.at[head, pl.ds(r * held, held)]
        return pltpu.make_async_remote_copy(
            src_ref=rows, dst_ref=rows, send_sem=att_send.at[head, r],
            recv_sem=att_recv.at[head, r], device_id={"tp": to}, device_id_type=MESH,
        )

    def multiply(head, q):
        block = piece_block(q)
        x = xn[pl.ds(block, 2)].reshape(step_rows, width)
        part[...] = jnp.dot(x, wbuf[head], preferred_element_type=jnp.float32)
        return pl.ds(pl.multiple_of(block * own_rows, step_rows), step_rows)

    def scale_block(block):
        x = xg[block].astype(jnp.float32)
        xn[block] = (x * gain_ref[...]).astype(jnp.bfloat16)
        x = x * x
        total = x[:, :HEAD]
        for t in range(1, width // HEAD):
            total += x[:, t * HEAD:(t + 1) * HEAD]
        squares[block] = total

    def begin(q):
        def scale(k, c):
            scale_block(piece_block(q) + k)
            return c

        lax.fori_loop(0, 2, scale, 0)

        @pl.when((tp == 0) | (tp == last))
        def _():
            def one_head(j, c):
                head = first * per_way + j
                if q == 0:
                    for kind in range(3):
                        weight_copy(head, kind).wait()
                at = multiply(head, q)
                buf[head, at, :] = part[...].astype(jnp.bfloat16)
                part_copy(head, q, tp + 2 * first - 1).start()
                return c

            lax.fori_loop(0, group, one_head, 0)

    across = other * n_cp + cp
    wait_rows(mine + 1 - 2 * core)
    begin(0)
    wait_rows(across)
    for m in mates:
        send_rows(xg.at[across], across, {"cp": m})
    send_rows(xg.at[across], across, {"cp": sibling})
    for k in range(1, pairs):
        block = sec * n_cp + ((pair + pairs - k) % pairs) * 2 + core
        wait_rows(block)
        send_rows(xg.at[block], block, {"cp": sibling})
    wait_rows(across + 1 - 2 * core)
    begin(1)
    for k in range(1, pairs):
        block = other * n_cp + ((pair + pairs - k) % pairs) * 2 + core
        wait_rows(block)
        send_rows(xg.at[block], block, {"cp": sibling})
    for k in range(1, pairs):
        for i, side in enumerate((sec, other)):
            wait_rows(side * n_cp + ((pair + pairs - k) % pairs) * 2 + 1 - core)
            begin(2 * k + i)

    summed = jnp.sum(squares[...].reshape(tokens, HEAD).T, axis=0, keepdims=True)
    square_rows[tp] = jnp.broadcast_to(summed, (8, tokens))
    square_copies = []
    for k in range(1, n_tp):
        copy = pltpu.make_async_remote_copy(
            src_ref=square_rows.at[tp], dst_ref=square_rows.at[tp], send_sem=sq_send.at[k - 1],
            recv_sem=sq_recv.at[tp], device_id={"tp": (tp + k) % n_tp}, device_id_type=MESH,
        )
        copy.start()
        square_copies.append(copy)

    def attend(head, back):
        def normalise(r, carry):
            at = pl.ds(pl.multiple_of(r * query_rows, query_rows), query_rows)
            inv = inv_cols[at, :]
            keys[at, :] = (buf[head, at, HEAD:2 * HEAD].astype(jnp.float32) * inv).astype(jnp.bfloat16)
            values[at, :] = (buf[head, at, 2 * HEAD:].astype(jnp.float32) * inv).astype(jnp.bfloat16)
            return carry

        lax.fori_loop(0, tokens // query_rows, normalise, 0)

        def queries(r, carry):
            at = pl.ds(pl.multiple_of(r * query_rows, query_rows), query_rows)
            q = (buf[head, at, :HEAD].astype(jnp.float32) * inv_cols[at, :]).astype(jnp.bfloat16)
            scores = lax.dot_general(
                q, keys[...], (((1,), (1,)), ((), ())), preferred_element_type=jnp.float32
            ) * (1.0 / math.sqrt(HEAD))
            spot = pos_k[...]
            allowed = (spot <= pos_q[at, :]) & (spot >= start_q[at, :])
            scores = jnp.where(allowed, scores, -1e30)
            peak = jnp.max(scores, axis=1, keepdims=True)
            weights = jnp.where(allowed, jnp.exp(scores - peak), 0.0)
            total = jnp.sum(weights, axis=1, keepdims=True)
            mixed = jnp.dot(
                weights.astype(jnp.bfloat16), values[...], preferred_element_type=jnp.float32
            )
            held = query_rows // own_rows
            att_ref[head, pl.ds(r * held, held)] = (
                (mixed / total).astype(jnp.bfloat16).reshape(held, own_rows, HEAD)
            )
            att_copy(head, r, back).start()
            return carry

        lax.fori_loop(0, tokens // query_rows, queries, 0)

    def slot(s, carry):
        @pl.when(s == 2)
        def _():
            for k in range(1, n_tp):
                src = (tp + k) % n_tp
                pltpu.make_async_remote_copy(
                    src_ref=square_rows.at[src], dst_ref=square_rows.at[src],
                    send_sem=sq_send.at[0], recv_sem=sq_recv.at[src],
                    device_id={"tp": src}, device_id_type=MESH,
                ).wait_recv()
            total = square_rows[0]
            for k in range(1, n_tp):
                total += square_rows[k]
            inv = lax.rsqrt(total[:1] / (width * n_tp) + 1e-05)
            inv_cols[...] = jnp.broadcast_to(inv, (HEAD, tokens)).T

        def partial_sums(o, c):
            way = (first + o) % 2
            place = way * tp + (1 - way) * (last - tp)
            onward, back = tp + 2 * way - 1, tp - 2 * way + 1

            @pl.when(place == 0)
            def _():
                i = s + ahead

                @pl.when((i >= lead) & (i < steps))
                def _():
                    head, q = decode(i)
                    head = way * per_way + head

                    @pl.when(q == 0)
                    def _():
                        for kind in range(3):
                            weight_copy(head, kind).wait()

                    at = multiply(head, q)
                    buf[head, at, :] = part[...].astype(jnp.bfloat16)
                    part_copy(head, q, onward).start()

            @pl.when(place > 0)
            def _():
                i = s - (place - 1) * hop

                @pl.when((i >= 0) & (i < steps))
                def _():
                    head, q = decode(i)
                    head = way * per_way + head

                    @pl.when(q == 0)
                    def _():
                        for kind in range(3):
                            weight_copy(head, kind).wait()

                    at = multiply(head, q)
                    part_copy(head, q, back).wait_recv()
                    held_sum = buf[head, at, :].astype(jnp.float32)
                    buf[head, at, :] = (held_sum + part[...]).astype(jnp.bfloat16)

                    @pl.when(place < last)
                    def _():
                        part_copy(head, q, onward).start()

            return c

        lax.fori_loop(0, 2, partial_sums, 0)

        def attended_rows(o, c):
            way = (first + 1 + o) % 2
            place = way * tp + (1 - way) * (last - tp)
            onward, back = tp + 2 * way - 1, tp - 2 * way + 1
            i = s - (last - 1) * hop - (last - place) * back_hop

            @pl.when((i >= 0) & (i < steps))
            def _():
                head, q = decode(i)
                head = way * per_way + head

                @pl.when(q == pieces - 1)
                def _():
                    @pl.when(place == last)
                    def _():
                        attend(head, back)

                    @pl.when(place < last)
                    def _():
                        def pass_on(r, d):
                            att_copy(head, r, onward).wait_recv()

                            @pl.when(place > 0)
                            def _():
                                att_copy(head, r, back).start()

                            return d

                        lax.fori_loop(0, att_pieces, pass_on, 0)

            return c

        lax.fori_loop(0, 2, attended_rows, 0)
        return carry

    steps = per_way * pieces
    hop, back_hop, ahead = 3, 6, min(4, lead)

    def decode(i):
        early = i < lead
        return (
            jnp.where(early, i % group, i // pieces),
            jnp.where(early, i // group, i % pieces),
        )

    lax.fori_loop(0, steps + (last - 1) * hop + last * back_hop, slot, 0)

    out_copy.wait()
    columns = lhs.shape[1]
    tile = min(width, 512)

    def project(section, to_core, target, arrived):
        for k in range(pairs):
            block = section * n_cp + 2 * k + to_core
            for h in range(heads):
                lhs[k * own_rows:(k + 1) * own_rows, h * HEAD:(h + 1) * HEAD] = att_ref[h, block]

        def one_tile(t, c):
            at = pl.ds(pl.multiple_of(t * tile, tile), tile)
            product = jnp.dot(
                lhs[...], w_out_buf[:, at], preferred_element_type=jnp.float32
            ).reshape(pairs, own_rows, tile)
            if arrived is not None:
                product += arrived[section, :, :, at].astype(jnp.float32)
            target[section, :, :, at] = product.astype(jnp.bfloat16)
            return c

        lax.fori_loop(0, width // tile, one_tile, 0)

    def pair_copy(section):
        return pltpu.make_async_remote_copy(
            src_ref=pair_out.at[section], dst_ref=pair_in.at[section],
            send_sem=pair_send.at[section], recv_sem=pair_recv.at[section],
            device_id={"cp": sibling}, device_id_type=MESH,
        )

    def mate_copy(section, k):
        to = (pair + k) % pairs
        return pltpu.make_async_remote_copy(
            src_ref=sums.at[section, to], dst_ref=mate_in.at[section, pair],
            send_sem=mate_send.at[section, to], recv_sem=mate_recv.at[section, pair],
            device_id={"cp": 2 * to + core}, device_id_type=MESH,
        )

    def wait_mate(section, k):
        src = (pair + pairs - k) % pairs
        pltpu.make_async_remote_copy(
            src_ref=mate_in.at[section, src], dst_ref=mate_in.at[section, src],
            send_sem=mate_send.at[section, src], recv_sem=mate_recv.at[section, src],
            device_id={"cp": 2 * src + core}, device_id_type=MESH,
        ).wait_recv()

    def total_of(section):
        total = sums[section, pair].astype(jnp.float32)
        for k in range(1, pairs):
            wait_mate(section, k)
            total += mate_in[section, (pair + pairs - k) % pairs].astype(jnp.float32)
        return total.astype(jnp.bfloat16)

    for section in (other, sec):
        project(section, 1 - core, pair_out, None)
        pair_copy(section).start()
        pair_copy(section).wait_recv()
        project(section, core, sums, pair_in)
        for k in range(1, pairs):
            mate_copy(section, k).start()

    over[...] = total_of(other)
    home = pltpu.make_async_remote_copy(
        src_ref=over, dst_ref=out_ref.at[sec], send_sem=home_send, recv_sem=home_recv,
        device_id={"section": other}, device_id_type=MESH,
    )
    home.start()
    out_ref[sec] = total_of(sec)
    home.wait()
    for section in (other, sec):
        pair_copy(section).wait_send()
        for k in range(1, pairs):
            mate_copy(section, k).wait_send()

    def finish(i, carry):
        for way in range(2):
            place = last - tp if way == 0 else tp
            onward = tp - 1 if way == 0 else tp + 1
            back = tp + 1 if way == 0 else tp - 1
            head = way * per_way + i

            @pl.when(place < last)
            def _():
                for piece in range(pieces):
                    part_copy(head, piece, onward).wait_send()

            @pl.when(place > 0)
            def _():
                for r in range(att_pieces):
                    att_copy(head, r, back).wait_send()

        return carry

    lax.fori_loop(0, per_way, finish, 0)
    for copy in sent + square_copies:
        copy.wait_send()


def on_device(rollout_rows, lengths, block_owner, norm_gain, w_qkv, w_out):
    n_tp, n_cp, n_sec = lax.axis_size("tp"), lax.axis_size("cp"), lax.axis_size("section")
    own_rows, width = rollout_rows.shape
    blocks = n_sec * n_cp
    tokens = own_rows * blocks
    columns = w_qkv.shape[3]
    heads = columns // HEAD
    bf16, f32 = jnp.bfloat16, jnp.float32
    sends = 2 + 2 * n_cp
    vmem = pl.BlockSpec(memory_space=pltpu.VMEM)
    smem = pl.BlockSpec(memory_space=pltpu.SMEM)
    dma = pltpu.SemaphoreType.DMA
    pairs = n_cp // 2
    pieces = n_sec * pairs
    att_pieces = tokens // min(tokens, 256)
    exchange = pltpu.VMEM((n_sec, pairs, own_rows, width), bf16)
    return pl.pallas_call(
        functools.partial(attend_kernel, n_sec, n_cp, n_tp),
        out_shape=jax.ShapeDtypeStruct((n_sec, own_rows, width), bf16),
        in_specs=[vmem, vmem, smem, smem] + [pl.BlockSpec(memory_space=pl.ANY)] * 2,
        out_specs=vmem,
        scratch_shapes=[
            pltpu.VMEM((heads, blocks, own_rows, HEAD), bf16),
            pltpu.VMEM((columns, width), bf16),
            pltpu.VMEM((pairs * own_rows, columns), bf16),
            exchange,
            exchange,
            exchange,
            exchange,
            pltpu.VMEM((own_rows, width), bf16),
            pltpu.VMEM((blocks, own_rows, width), bf16),
            pltpu.VMEM((blocks, own_rows, width), bf16),
            pltpu.VMEM((heads, width, 3 * HEAD), bf16),
            pltpu.VMEM((heads, tokens, 3 * HEAD), bf16),
            pltpu.VMEM((2 * own_rows, 3 * HEAD), f32),
            pltpu.VMEM((blocks, own_rows, HEAD), f32),
            pltpu.VMEM((n_tp, 8, tokens), f32),
            pltpu.VMEM((tokens, HEAD), f32),
            pltpu.VMEM((tokens, HEAD), bf16),
            pltpu.VMEM((tokens, HEAD), bf16),
            pltpu.VMEM((tokens, 1), jnp.int32),
            pltpu.VMEM((tokens, 1), jnp.int32),
            pltpu.VMEM((1, tokens), jnp.int32),
            dma((heads, 3)),
            dma((sends,)),
            dma((blocks,)),
            dma((n_tp,)),
            dma((n_tp,)),
            dma((heads, pieces)),
            dma((heads, pieces)),
            dma((heads, att_pieces)),
            dma((heads, att_pieces)),
            dma,
            dma((n_sec,)),
            dma((n_sec,)),
            dma((n_sec, pairs)),
            dma((n_sec, pairs)),
            dma,
            dma,
        ],
        compiler_params=pltpu.CompilerParams(
            collective_id=0, has_side_effects=True, vmem_limit_bytes=62 * 1024 * 1024
        ),
        name="attend",
    )(rollout_rows, norm_gain, block_owner, lengths, w_qkv, w_out)


def solution(mesh):
    return jax.shard_map(
        on_device,
        mesh=mesh,
        in_specs=(
            P(("section", "cp"), "tp"),
            P(),
            P(),
            P("section", "tp"),
            P("section", None, "tp", "cp"),
            P("section", "cp", "tp"),
        ),
        out_specs=P(None, ("section", "cp"), "tp"),
        check_vma=False,
    )
```

```python
import functools
import math

import jax
import jax.numpy as jnp
from jax import lax
from jax.experimental import pallas as pl
from jax.experimental.pallas import tpu as pltpu
from jax.sharding import PartitionSpec as P

HEAD = 128
MESH = pl.DeviceIdType.MESH


def attend_kernel(
    n_sec, n_cp, n_tp,
    rows_ref, gain_ref, owner_ref, lengths_ref, w_ref, w_out_ref,
    out_ref,
    att_ref, w_out_buf, lhs, pair_out, pair_in, sums, mate_in, over,
    xg, xn, wbuf, buf, part, squares, square_rows, inv_cols, keys, values, pos_q, start_q, pos_k,
    w_sem, row_send, row_recv, sq_send, sq_recv, part_send, part_recv, att_send, att_recv,
    out_sem, pair_send, pair_recv, mate_send, mate_recv, home_send, home_recv,
):
    sec, cp, tp = lax.axis_index("section"), lax.axis_index("cp"), lax.axis_index("tp")
    blocks, own_rows, width = xg.shape
    tokens = blocks * own_rows
    heads = buf.shape[0]
    per_way = heads // 2
    last = n_tp - 1
    pairs = n_cp // 2
    pair, core = cp // 2, cp % 2
    sibling = cp + 1 - 2 * core
    other = 1 - sec
    mine = sec * n_cp + cp

    def weight_copy(head, kind):
        return pltpu.make_async_copy(
            w_ref.at[0, kind, :, pl.ds(pl.multiple_of(head * HEAD, HEAD), HEAD)],
            wbuf.at[head, :, pl.ds(kind * HEAD, HEAD)],
            w_sem.at[head, kind],
        )

    for i in range(per_way):
        for way in range(2):
            for kind in range(3):
                weight_copy(way * per_way + i, kind).start()

    out_copy = pltpu.make_async_copy(w_out_ref.at[0], w_out_buf, out_sem)
    out_copy.start()

    mates = [((pair + k) % pairs) * 2 + core for k in range(1, pairs)]
    barrier = pltpu.get_barrier_semaphore()
    peers = [{"section": other}, {"cp": sibling}]
    peers += [{"cp": m} for m in mates]
    peers += [{"tp": (tp + k) % n_tp} for k in range(1, n_tp)]
    for peer in peers:
        pl.semaphore_signal(barrier, inc=1, device_id=peer, device_id_type=MESH)
    pl.semaphore_wait(barrier, len(peers))

    sent = []

    def send_rows(src, block, peer):
        copy = pltpu.make_async_remote_copy(
            src_ref=src, dst_ref=xg.at[block], send_sem=row_send.at[len(sent)],
            recv_sem=row_recv.at[block], device_id=peer, device_id_type=MESH,
        )
        copy.start()
        sent.append(copy)

    def wait_rows(block):
        pltpu.make_async_remote_copy(
            src_ref=xg.at[block], dst_ref=xg.at[block], send_sem=row_send.at[0],
            recv_sem=row_recv.at[block], device_id={"cp": sibling}, device_id_type=MESH,
        ).wait_recv()

    send_rows(rows_ref, mine, {"section": other})
    for m in mates:
        send_rows(rows_ref, mine, {"cp": m})
    send_rows(rows_ref, mine, {"cp": sibling})
    xg[mine] = rows_ref[...]

    def positions(shape, dim):
        row = lax.broadcasted_iota(jnp.int32, shape, dim)
        pos = jnp.zeros(shape, jnp.int32)
        for b in range(blocks):
            off = row - owner_ref[b] * own_rows
            pos = jnp.where((off >= 0) & (off < own_rows), off + b * own_rows, pos)
        return pos

    pos = positions((tokens, 1), 0)
    pos_q[...] = pos
    start = jnp.zeros((tokens, 1), jnp.int32)
    end = lengths_ref[0]
    for i in range(1, lengths_ref.shape[0] + 1):
        start = jnp.where(pos >= end, end, start)
        if i < lengths_ref.shape[0]:
            end = end + lengths_ref[i]
    start_q[...] = start
    pos_k[...] = positions((1, tokens), 1)

    pieces = n_sec * pairs
    step_rows = 2 * own_rows
    query_rows = min(tokens, 256)
    att_pieces = tokens // query_rows
    group = min(2, per_way)
    lead = group * pieces
    first = 1 - (2 * tp) // n_tp

    def piece_block(q):
        section = sec + (q % 2) * (other - sec)
        return section * n_cp + 2 * ((pair + pairs - q // 2) % pairs)

    def part_copy(head, q, to):
        rows = buf.at[head, pl.ds(pl.multiple_of(piece_block(q) * own_rows, step_rows), step_rows)]
        return pltpu.make_async_remote_copy(
            src_ref=rows, dst_ref=rows, send_sem=part_send.at[head, q],
            recv_sem=part_recv.at[head, q], device_id={"tp": to}, device_id_type=MESH,
        )

    def att_copy(head, r, to):
        held = query_rows // own_rows
        rows = att_ref.at[head, pl.ds(r * held, held)]
        return pltpu.make_async_remote_copy(
            src_ref=rows, dst_ref=rows, send_sem=att_send.at[head, r],
            recv_sem=att_recv.at[head, r], device_id={"tp": to}, device_id_type=MESH,
        )

    def multiply(head, q):
        block = piece_block(q)
        x = xn[pl.ds(block, 2)].reshape(step_rows, width)
        part[...] = jnp.dot(x, wbuf[head], preferred_element_type=jnp.float32)
        return pl.ds(pl.multiple_of(block * own_rows, step_rows), step_rows)

    def scale_block(block):
        x = xg[block].astype(jnp.float32)
        xn[block] = (x * gain_ref[...]).astype(jnp.bfloat16)
        x = x * x
        total = x[:, :HEAD]
        for t in range(1, width // HEAD):
            total += x[:, t * HEAD:(t + 1) * HEAD]
        squares[block] = total

    def begin(q):
        def scale(k, c):
            scale_block(piece_block(q) + k)
            return c

        lax.fori_loop(0, 2, scale, 0)

        @pl.when((tp == 0) | (tp == last))
        def _():
            def one_head(j, c):
                head = first * per_way + j
                if q == 0:
                    for kind in range(3):
                        weight_copy(head, kind).wait()
                at = multiply(head, q)
                buf[head, at, :] = part[...].astype(jnp.bfloat16)
                part_copy(head, q, tp + 2 * first - 1).start()
                return c

            lax.fori_loop(0, group, one_head, 0)

    across = other * n_cp + cp
    wait_rows(mine + 1 - 2 * core)
    begin(0)
    wait_rows(across)
    for m in mates:
        send_rows(xg.at[across], across, {"cp": m})
    send_rows(xg.at[across], across, {"cp": sibling})
    for k in range(1, pairs):
        block = sec * n_cp + ((pair + pairs - k) % pairs) * 2 + core
        wait_rows(block)
        send_rows(xg.at[block], block, {"cp": sibling})
    wait_rows(across + 1 - 2 * core)
    begin(1)
    for k in range(1, pairs):
        block = other * n_cp + ((pair + pairs - k) % pairs) * 2 + core
        wait_rows(block)
        send_rows(xg.at[block], block, {"cp": sibling})
    for k in range(1, pairs):
        for i, side in enumerate((sec, other)):
            wait_rows(side * n_cp + ((pair + pairs - k) % pairs) * 2 + 1 - core)
            begin(2 * k + i)

    summed = jnp.sum(squares[...].reshape(tokens, HEAD).T, axis=0, keepdims=True)
    square_rows[tp] = jnp.broadcast_to(summed, (8, tokens))
    square_copies = []
    for k in range(1, n_tp):
        copy = pltpu.make_async_remote_copy(
            src_ref=square_rows.at[tp], dst_ref=square_rows.at[tp], send_sem=sq_send.at[k - 1],
            recv_sem=sq_recv.at[tp], device_id={"tp": (tp + k) % n_tp}, device_id_type=MESH,
        )
        copy.start()
        square_copies.append(copy)

    def attend(head, back):
        def normalise(r, carry):
            at = pl.ds(pl.multiple_of(r * query_rows, query_rows), query_rows)
            inv = inv_cols[at, :]
            keys[at, :] = (buf[head, at, HEAD:2 * HEAD].astype(jnp.float32) * inv).astype(jnp.bfloat16)
            values[at, :] = (buf[head, at, 2 * HEAD:].astype(jnp.float32) * inv).astype(jnp.bfloat16)
            return carry

        lax.fori_loop(0, tokens // query_rows, normalise, 0)

        def queries(r, carry):
            at = pl.ds(pl.multiple_of(r * query_rows, query_rows), query_rows)
            q = (buf[head, at, :HEAD].astype(jnp.float32) * inv_cols[at, :]).astype(jnp.bfloat16)
            scores = lax.dot_general(
                q, keys[...], (((1,), (1,)), ((), ())), preferred_element_type=jnp.float32
            ) * (1.0 / math.sqrt(HEAD))
            spot = pos_k[...]
            allowed = (spot <= pos_q[at, :]) & (spot >= start_q[at, :])
            scores = jnp.where(allowed, scores, -1e30)
            peak = jnp.max(scores, axis=1, keepdims=True)
            weights = jnp.where(allowed, jnp.exp(scores - peak), 0.0)
            total = jnp.sum(weights, axis=1, keepdims=True)
            mixed = jnp.dot(
                weights.astype(jnp.bfloat16), values[...], preferred_element_type=jnp.float32
            )
            held = query_rows // own_rows
            att_ref[head, pl.ds(r * held, held)] = (
                (mixed / total).astype(jnp.bfloat16).reshape(held, own_rows, HEAD)
            )
            att_copy(head, r, back).start()
            return carry

        lax.fori_loop(0, tokens // query_rows, queries, 0)

    def slot(s, carry):
        @pl.when(s == 2)
        def _():
            for k in range(1, n_tp):
                src = (tp + k) % n_tp
                pltpu.make_async_remote_copy(
                    src_ref=square_rows.at[src], dst_ref=square_rows.at[src],
                    send_sem=sq_send.at[0], recv_sem=sq_recv.at[src],
                    device_id={"tp": src}, device_id_type=MESH,
                ).wait_recv()
            total = square_rows[0]
            for k in range(1, n_tp):
                total += square_rows[k]
            inv = lax.rsqrt(total[:1] / (width * n_tp) + 1e-05)
            inv_cols[...] = jnp.broadcast_to(inv, (HEAD, tokens)).T

        def partial_sums(o, c):
            way = (first + o) % 2
            place = way * tp + (1 - way) * (last - tp)
            onward, back = tp + 2 * way - 1, tp - 2 * way + 1

            @pl.when(place == 0)
            def _():
                i = s + ahead

                @pl.when((i >= lead) & (i < steps))
                def _():
                    head, q = decode(i)
                    head = way * per_way + head

                    @pl.when(q == 0)
                    def _():
                        for kind in range(3):
                            weight_copy(head, kind).wait()

                    at = multiply(head, q)
                    buf[head, at, :] = part[...].astype(jnp.bfloat16)
                    part_copy(head, q, onward).start()

            @pl.when(place > 0)
            def _():
                i = s - (place - 1) * hop

                @pl.when((i >= 0) & (i < steps))
                def _():
                    head, q = decode(i)
                    head = way * per_way + head

                    @pl.when(q == 0)
                    def _():
                        for kind in range(3):
                            weight_copy(head, kind).wait()

                    at = multiply(head, q)
                    part_copy(head, q, back).wait_recv()
                    held_sum = buf[head, at, :].astype(jnp.float32)
                    buf[head, at, :] = (held_sum + part[...]).astype(jnp.bfloat16)

                    @pl.when(place < last)
                    def _():
                        part_copy(head, q, onward).start()

            return c

        lax.fori_loop(0, 2, partial_sums, 0)

        def attended_rows(o, c):
            way = (first + 1 + o) % 2
            place = way * tp + (1 - way) * (last - tp)
            onward, back = tp + 2 * way - 1, tp - 2 * way + 1
            i = s - (last - 1) * hop - (last - place) * back_hop

            @pl.when((i >= 0) & (i < steps))
            def _():
                head, q = decode(i)
                head = way * per_way + head

                @pl.when(q == pieces - 1)
                def _():
                    @pl.when(place == last)
                    def _():
                        attend(head, back)

                    @pl.when(place < last)
                    def _():
                        def pass_on(r, d):
                            att_copy(head, r, onward).wait_recv()

                            @pl.when(place > 0)
                            def _():
                                att_copy(head, r, back).start()

                            return d

                        lax.fori_loop(0, att_pieces, pass_on, 0)

            return c

        lax.fori_loop(0, 2, attended_rows, 0)
        return carry

    steps = per_way * pieces
    hop, back_hop, ahead = 3, 4, min(3, lead)

    def decode(i):
        early = i < lead
        return (
            jnp.where(early, i % group, i // pieces),
            jnp.where(early, i // group, i % pieces),
        )

    lax.fori_loop(0, steps + (last - 1) * hop + last * back_hop, slot, 0)

    out_copy.wait()
    half_width = width // 2
    tile = min(half_width, 512)

    def gather_heads(section, to_core):
        for k in range(pairs):
            block = section * n_cp + 2 * k + to_core
            for h in range(heads):
                lhs[section, to_core, k * own_rows:(k + 1) * own_rows, h * HEAD:(h + 1) * HEAD] = (
                    att_ref[h, block]
                )

    def project(section, half, to_core, target, arrived):
        def one_tile(t, c):
            at = pl.ds(pl.multiple_of(t * tile, tile), tile)
            columns = pl.ds(pl.multiple_of(half * half_width + t * tile, tile), tile)
            product = jnp.dot(
                lhs[section, to_core], w_out_buf[:, columns], preferred_element_type=jnp.float32
            ).reshape(pairs, own_rows, tile)
            if arrived is not None:
                product += arrived[section, half, :, :, at].astype(jnp.float32)
            target[section, half, :, :, at] = product.astype(jnp.bfloat16)
            return c

        lax.fori_loop(0, half_width // tile, one_tile, 0)

    def pair_copy(section, half):
        return pltpu.make_async_remote_copy(
            src_ref=pair_out.at[section, half], dst_ref=pair_in.at[section, half],
            send_sem=pair_send.at[section, half], recv_sem=pair_recv.at[section, half],
            device_id={"cp": sibling}, device_id_type=MESH,
        )

    def mate_copy(section, half, k):
        to = (pair + k) % pairs
        return pltpu.make_async_remote_copy(
            src_ref=sums.at[section, half, to], dst_ref=mate_in.at[section, half, pair],
            send_sem=mate_send.at[section, half, to], recv_sem=mate_recv.at[section, half, pair],
            device_id={"cp": 2 * to + core}, device_id_type=MESH,
        )

    def wait_mate(section, half, k):
        src = (pair + pairs - k) % pairs
        pltpu.make_async_remote_copy(
            src_ref=mate_in.at[section, half, src], dst_ref=mate_in.at[section, half, src],
            send_sem=mate_send.at[section, half, src], recv_sem=mate_recv.at[section, half, src],
            device_id={"cp": 2 * src + core}, device_id_type=MESH,
        ).wait_recv()

    def total_of(section, half):
        total = sums[section, half, pair].astype(jnp.float32)
        for k in range(1, pairs):
            wait_mate(section, half, k)
            total += mate_in[section, half, (pair + pairs - k) % pairs].astype(jnp.float32)
        return total.astype(jnp.bfloat16)

    def to_sibling(section, half):
        if half == 0:
            gather_heads(section, 1 - core)
        project(section, half, 1 - core, pair_out, None)
        pair_copy(section, half).start()

    def to_mates(section, half):
        if half == 0:
            gather_heads(section, core)
        pair_copy(section, half).wait_recv()
        project(section, half, core, sums, pair_in)
        for k in range(1, pairs):
            mate_copy(section, half, k).start()

    order = [(other, 0), (other, 1), (sec, 0), (sec, 1)]
    to_sibling(*order[0])
    for n, spot in enumerate(order):
        if n + 1 < len(order):
            to_sibling(*order[n + 1])
        to_mates(*spot)

    homes = []
    for half in range(2):
        over[half] = total_of(other, half)
        home = pltpu.make_async_remote_copy(
            src_ref=over.at[half],
            dst_ref=out_ref.at[sec, :, pl.ds(half * half_width, half_width)],
            send_sem=home_send.at[half], recv_sem=home_recv.at[half],
            device_id={"section": other}, device_id_type=MESH,
        )
        home.start()
        homes.append(home)
    for half in range(2):
        out_ref[sec, :, half * half_width:(half + 1) * half_width] = total_of(sec, half)
    for home in homes:
        home.wait()
    for section, half in order:
        pair_copy(section, half).wait_send()
        for k in range(1, pairs):
            mate_copy(section, half, k).wait_send()

    def finish(i, carry):
        for way in range(2):
            place = last - tp if way == 0 else tp
            onward = tp - 1 if way == 0 else tp + 1
            back = tp + 1 if way == 0 else tp - 1
            head = way * per_way + i

            @pl.when(place < last)
            def _():
                for piece in range(pieces):
                    part_copy(head, piece, onward).wait_send()

            @pl.when(place > 0)
            def _():
                for r in range(att_pieces):
                    att_copy(head, r, back).wait_send()

        return carry

    lax.fori_loop(0, per_way, finish, 0)
    for copy in sent + square_copies:
        copy.wait_send()


def on_device(rollout_rows, lengths, block_owner, norm_gain, w_qkv, w_out):
    n_tp, n_cp, n_sec = lax.axis_size("tp"), lax.axis_size("cp"), lax.axis_size("section")
    own_rows, width = rollout_rows.shape
    blocks = n_sec * n_cp
    tokens = own_rows * blocks
    columns = w_qkv.shape[3]
    heads = columns // HEAD
    bf16, f32 = jnp.bfloat16, jnp.float32
    sends = 2 + 2 * n_cp
    vmem = pl.BlockSpec(memory_space=pltpu.VMEM)
    smem = pl.BlockSpec(memory_space=pltpu.SMEM)
    dma = pltpu.SemaphoreType.DMA
    pairs = n_cp // 2
    pieces = n_sec * pairs
    att_pieces = tokens // min(tokens, 256)
    exchange = pltpu.VMEM((n_sec, 2, pairs, own_rows, width // 2), bf16)
    return pl.pallas_call(
        functools.partial(attend_kernel, n_sec, n_cp, n_tp),
        out_shape=jax.ShapeDtypeStruct((n_sec, own_rows, width), bf16),
        in_specs=[vmem, vmem, smem, smem] + [pl.BlockSpec(memory_space=pl.ANY)] * 2,
        out_specs=vmem,
        scratch_shapes=[
            pltpu.VMEM((heads, blocks, own_rows, HEAD), bf16),
            pltpu.VMEM((columns, width), bf16),
            pltpu.VMEM((n_sec, 2, pairs * own_rows, columns), bf16),
            exchange,
            exchange,
            exchange,
            exchange,
            pltpu.VMEM((2, own_rows, width // 2), bf16),
            pltpu.VMEM((blocks, own_rows, width), bf16),
            pltpu.VMEM((blocks, own_rows, width), bf16),
            pltpu.VMEM((heads, width, 3 * HEAD), bf16),
            pltpu.VMEM((heads, tokens, 3 * HEAD), bf16),
            pltpu.VMEM((2 * own_rows, 3 * HEAD), f32),
            pltpu.VMEM((blocks, own_rows, HEAD), f32),
            pltpu.VMEM((n_tp, 8, tokens), f32),
            pltpu.VMEM((tokens, HEAD), f32),
            pltpu.VMEM((tokens, HEAD), bf16),
            pltpu.VMEM((tokens, HEAD), bf16),
            pltpu.VMEM((tokens, 1), jnp.int32),
            pltpu.VMEM((tokens, 1), jnp.int32),
            pltpu.VMEM((1, tokens), jnp.int32),
            dma((heads, 3)),
            dma((sends,)),
            dma((blocks,)),
            dma((n_tp,)),
            dma((n_tp,)),
            dma((heads, pieces)),
            dma((heads, pieces)),
            dma((heads, att_pieces)),
            dma((heads, att_pieces)),
            dma,
            dma((n_sec, 2)),
            dma((n_sec, 2)),
            dma((n_sec, 2, pairs)),
            dma((n_sec, 2, pairs)),
            dma((2,)),
            dma((2,)),
        ],
        compiler_params=pltpu.CompilerParams(
            collective_id=0, has_side_effects=True, vmem_limit_bytes=62 * 1024 * 1024
        ),
        name="attend",
    )(rollout_rows, norm_gain, block_owner, lengths, w_qkv, w_out)


def solution(mesh):
    return jax.shard_map(
        on_device,
        mesh=mesh,
        in_specs=(
            P(("section", "cp"), "tp"),
            P(),
            P(),
            P("section", "tp"),
            P("section", None, "tp", "cp"),
            P("section", "cp", "tp"),
        ),
        out_specs=P(None, ("section", "cp"), "tp"),
        check_vma=False,
    )
```

```python
import functools
import math

import jax
import jax.numpy as jnp
from jax import lax
from jax.experimental import pallas as pl
from jax.experimental.pallas import tpu as pltpu
from jax.sharding import PartitionSpec as P

HEAD = 128
MESH = pl.DeviceIdType.MESH


def attend_kernel(
    n_sec, n_cp, n_tp,
    rows_ref, gain_ref, owner_ref, lengths_ref, w_ref, w_out_ref,
    out_ref,
    att_ref, w_out_buf, lhs, pair_out, pair_in, sums, mate_in, over,
    xg, xn, wbuf, buf, part, squares, square_rows, inv_cols, keys, values, pos_q, start_q, pos_k,
    w_sem, row_send, row_recv, sq_send, sq_recv, part_send, part_recv, att_send, att_recv,
    out_sem, pair_send, pair_recv, mate_send, mate_recv, home_send, home_recv,
):
    sec, cp, tp = lax.axis_index("section"), lax.axis_index("cp"), lax.axis_index("tp")
    blocks, own_rows, width = xg.shape
    tokens = blocks * own_rows
    heads = buf.shape[0]
    per_way = heads // 2
    last = n_tp - 1
    pairs = n_cp // 2
    pair, core = cp // 2, cp % 2
    sibling = cp + 1 - 2 * core
    other = 1 - sec
    mine = sec * n_cp + cp

    def weight_copy(head, kind):
        return pltpu.make_async_copy(
            w_ref.at[0, kind, :, pl.ds(pl.multiple_of(head * HEAD, HEAD), HEAD)],
            wbuf.at[head, :, pl.ds(kind * HEAD, HEAD)],
            w_sem.at[head, kind],
        )

    for i in range(per_way):
        for way in range(2):
            for kind in range(3):
                weight_copy(way * per_way + i, kind).start()

    out_copy = pltpu.make_async_copy(w_out_ref.at[0], w_out_buf, out_sem)
    out_copy.start()

    mates = [((pair + k) % pairs) * 2 + core for k in range(1, pairs)]
    barrier = pltpu.get_barrier_semaphore()
    peers = [{"section": other}, {"cp": sibling}]
    peers += [{"cp": m} for m in mates]
    peers += [{"tp": (tp + k) % n_tp} for k in range(1, n_tp)]
    for peer in peers:
        pl.semaphore_signal(barrier, inc=1, device_id=peer, device_id_type=MESH)
    pl.semaphore_wait(barrier, len(peers))

    sent = []

    def send_rows(src, block, peer):
        copy = pltpu.make_async_remote_copy(
            src_ref=src, dst_ref=xg.at[block], send_sem=row_send.at[len(sent)],
            recv_sem=row_recv.at[block], device_id=peer, device_id_type=MESH,
        )
        copy.start()
        sent.append(copy)

    def wait_rows(block):
        pltpu.make_async_remote_copy(
            src_ref=xg.at[block], dst_ref=xg.at[block], send_sem=row_send.at[0],
            recv_sem=row_recv.at[block], device_id={"cp": sibling}, device_id_type=MESH,
        ).wait_recv()

    send_rows(rows_ref, mine, {"section": other})
    for m in mates:
        send_rows(rows_ref, mine, {"cp": m})
    send_rows(rows_ref, mine, {"cp": sibling})
    xg[mine] = rows_ref[...]

    def positions(shape, dim):
        row = lax.broadcasted_iota(jnp.int32, shape, dim)
        pos = jnp.zeros(shape, jnp.int32)
        for b in range(blocks):
            off = row - owner_ref[b] * own_rows
            pos = jnp.where((off >= 0) & (off < own_rows), off + b * own_rows, pos)
        return pos

    pos = positions((tokens, 1), 0)
    pos_q[...] = pos
    start = jnp.zeros((tokens, 1), jnp.int32)
    end = lengths_ref[0]
    for i in range(1, lengths_ref.shape[0] + 1):
        start = jnp.where(pos >= end, end, start)
        if i < lengths_ref.shape[0]:
            end = end + lengths_ref[i]
    start_q[...] = start
    pos_k[...] = positions((1, tokens), 1)

    pieces = n_sec * pairs
    step_rows = 2 * own_rows
    query_rows = min(tokens, 256)
    att_pieces = tokens // query_rows
    group = min(2, per_way)
    lead = group * pieces
    first = 1 - (2 * tp) // n_tp

    def piece_block(q):
        section = sec + (q % 2) * (other - sec)
        return section * n_cp + 2 * ((pair + pairs - q // 2) % pairs)

    def part_copy(head, q, to):
        rows = buf.at[head, pl.ds(pl.multiple_of(piece_block(q) * own_rows, step_rows), step_rows)]
        return pltpu.make_async_remote_copy(
            src_ref=rows, dst_ref=rows, send_sem=part_send.at[head, q],
            recv_sem=part_recv.at[head, q], device_id={"tp": to}, device_id_type=MESH,
        )

    def att_copy(head, r, to):
        held = query_rows // own_rows
        rows = att_ref.at[head, pl.ds(r * held, held)]
        return pltpu.make_async_remote_copy(
            src_ref=rows, dst_ref=rows, send_sem=att_send.at[head, r],
            recv_sem=att_recv.at[head, r], device_id={"tp": to}, device_id_type=MESH,
        )

    def multiply(head, q):
        block = piece_block(q)
        x = xn[pl.ds(block, 2)].reshape(step_rows, width)
        part[...] = jnp.dot(x, wbuf[head], preferred_element_type=jnp.float32)
        return pl.ds(pl.multiple_of(block * own_rows, step_rows), step_rows)

    def scale_block(block):
        x = xg[block].astype(jnp.float32)
        xn[block] = (x * gain_ref[...]).astype(jnp.bfloat16)
        x = x * x
        total = x[:, :HEAD]
        for t in range(1, width // HEAD):
            total += x[:, t * HEAD:(t + 1) * HEAD]
        squares[block] = total

    def begin(q):
        def scale(k, c):
            scale_block(piece_block(q) + k)
            return c

        lax.fori_loop(0, 2, scale, 0)

        @pl.when((tp == 0) | (tp == last))
        def _():
            def one_head(j, c):
                head = first * per_way + j
                if q == 0:
                    for kind in range(3):
                        weight_copy(head, kind).wait()
                at = multiply(head, q)
                buf[head, at, :] = part[...].astype(jnp.bfloat16)
                part_copy(head, q, tp + 2 * first - 1).start()
                return c

            lax.fori_loop(0, group, one_head, 0)

    across = other * n_cp + cp
    wait_rows(mine + 1 - 2 * core)
    begin(0)
    wait_rows(across)
    for m in mates:
        send_rows(xg.at[across], across, {"cp": m})
    send_rows(xg.at[across], across, {"cp": sibling})
    for k in range(1, pairs):
        block = sec * n_cp + ((pair + pairs - k) % pairs) * 2 + core
        wait_rows(block)
        send_rows(xg.at[block], block, {"cp": sibling})
    wait_rows(across + 1 - 2 * core)
    begin(1)
    for k in range(1, pairs):
        block = other * n_cp + ((pair + pairs - k) % pairs) * 2 + core
        wait_rows(block)
        send_rows(xg.at[block], block, {"cp": sibling})
    for k in range(1, pairs):
        for i, side in enumerate((sec, other)):
            wait_rows(side * n_cp + ((pair + pairs - k) % pairs) * 2 + 1 - core)
            begin(2 * k + i)

    summed = jnp.sum(squares[...].reshape(tokens, HEAD).T, axis=0, keepdims=True)
    square_rows[tp] = jnp.broadcast_to(summed, (8, tokens))
    square_copies = []
    for k in range(1, n_tp):
        copy = pltpu.make_async_remote_copy(
            src_ref=square_rows.at[tp], dst_ref=square_rows.at[tp], send_sem=sq_send.at[k - 1],
            recv_sem=sq_recv.at[tp], device_id={"tp": (tp + k) % n_tp}, device_id_type=MESH,
        )
        copy.start()
        square_copies.append(copy)

    def attend(head, back):
        def normalise(r, carry):
            at = pl.ds(pl.multiple_of(r * query_rows, query_rows), query_rows)
            inv = inv_cols[at, :]
            keys[at, :] = (buf[head, at, HEAD:2 * HEAD].astype(jnp.float32) * inv).astype(jnp.bfloat16)
            values[at, :] = (buf[head, at, 2 * HEAD:].astype(jnp.float32) * inv).astype(jnp.bfloat16)
            return carry

        lax.fori_loop(0, tokens // query_rows, normalise, 0)

        def queries(r, carry):
            at = pl.ds(pl.multiple_of(r * query_rows, query_rows), query_rows)
            q = (buf[head, at, :HEAD].astype(jnp.float32) * inv_cols[at, :]).astype(jnp.bfloat16)
            scores = lax.dot_general(
                q, keys[...], (((1,), (1,)), ((), ())), preferred_element_type=jnp.float32
            )
            spot = pos_k[...]
            allowed = (spot <= pos_q[at, :]) & (spot >= start_q[at, :])
            scores = jnp.where(allowed, scores, -1e30)
            peak = jnp.max(scores, axis=1, keepdims=True)
            weights = jnp.exp2((scores - peak) * (math.log2(math.e) / math.sqrt(HEAD)))
            total = jnp.sum(weights, axis=1, keepdims=True)
            mixed = jnp.dot(
                weights.astype(jnp.bfloat16), values[...], preferred_element_type=jnp.float32
            )
            held = query_rows // own_rows
            att_ref[head, pl.ds(r * held, held)] = (
                (mixed / total).astype(jnp.bfloat16).reshape(held, own_rows, HEAD)
            )
            att_copy(head, r, back).start()
            return carry

        lax.fori_loop(0, tokens // query_rows, queries, 0)

    def slot(s, carry):
        @pl.when(s == 2)
        def _():
            for k in range(1, n_tp):
                src = (tp + k) % n_tp
                pltpu.make_async_remote_copy(
                    src_ref=square_rows.at[src], dst_ref=square_rows.at[src],
                    send_sem=sq_send.at[0], recv_sem=sq_recv.at[src],
                    device_id={"tp": src}, device_id_type=MESH,
                ).wait_recv()
            total = square_rows[0]
            for k in range(1, n_tp):
                total += square_rows[k]
            inv = lax.rsqrt(total[:1] / (width * n_tp) + 1e-05)
            inv_cols[...] = jnp.broadcast_to(inv, (HEAD, tokens)).T

        def partial_sums(o, c):
            way = (first + o) % 2
            place = way * tp + (1 - way) * (last - tp)
            onward, back = tp + 2 * way - 1, tp - 2 * way + 1

            @pl.when(place == 0)
            def _():
                i = s + ahead

                @pl.when((i >= lead) & (i < steps))
                def _():
                    head, q = decode(i)
                    head = way * per_way + head

                    @pl.when(q == 0)
                    def _():
                        for kind in range(3):
                            weight_copy(head, kind).wait()

                    at = multiply(head, q)
                    buf[head, at, :] = part[...].astype(jnp.bfloat16)
                    part_copy(head, q, onward).start()

            @pl.when(place > 0)
            def _():
                i = s - (place - 1) * hop

                @pl.when((i >= 0) & (i < steps))
                def _():
                    head, q = decode(i)
                    head = way * per_way + head

                    @pl.when(q == 0)
                    def _():
                        for kind in range(3):
                            weight_copy(head, kind).wait()

                    at = multiply(head, q)
                    part_copy(head, q, back).wait_recv()
                    held_sum = buf[head, at, :].astype(jnp.float32)
                    buf[head, at, :] = (held_sum + part[...]).astype(jnp.bfloat16)

                    @pl.when(place < last)
                    def _():
                        part_copy(head, q, onward).start()

            return c

        lax.fori_loop(0, 2, partial_sums, 0)

        def attended_rows(o, c):
            way = (first + 1 + o) % 2
            place = way * tp + (1 - way) * (last - tp)
            onward, back = tp + 2 * way - 1, tp - 2 * way + 1
            i = s - (last - 1) * hop - (last - place) * back_hop

            @pl.when((i >= 0) & (i < steps))
            def _():
                head, q = decode(i)
                head = way * per_way + head

                @pl.when(q == pieces - 1)
                def _():
                    @pl.when(place == last)
                    def _():
                        attend(head, back)

                    @pl.when(place < last)
                    def _():
                        def pass_on(r, d):
                            att_copy(head, r, onward).wait_recv()

                            @pl.when(place > 0)
                            def _():
                                att_copy(head, r, back).start()

                            return d

                        lax.fori_loop(0, att_pieces, pass_on, 0)

            return c

        lax.fori_loop(0, 2, attended_rows, 0)
        return carry

    steps = per_way * pieces
    hop, back_hop, ahead = 4, 4, min(4, lead)

    def decode(i):
        early = i < lead
        return (
            jnp.where(early, i % group, i // pieces),
            jnp.where(early, i // group, i % pieces),
        )

    lax.fori_loop(0, steps + (last - 1) * hop + last * back_hop, slot, 0)

    out_copy.wait()
    half_width = width // 2
    tile = min(half_width, 512)

    def gather_heads(section, to_core):
        for k in range(pairs):
            block = section * n_cp + 2 * k + to_core
            for h in range(heads):
                lhs[section, to_core, k * own_rows:(k + 1) * own_rows, h * HEAD:(h + 1) * HEAD] = (
                    att_ref[h, block]
                )

    def project(section, half, to_core, target, arrived):
        def one_tile(t, c):
            at = pl.ds(pl.multiple_of(t * tile, tile), tile)
            columns = pl.ds(pl.multiple_of(half * half_width + t * tile, tile), tile)
            product = jnp.dot(
                lhs[section, to_core], w_out_buf[:, columns], preferred_element_type=jnp.float32
            ).reshape(pairs, own_rows, tile)
            if arrived is not None:
                product += arrived[section, half, :, :, at].astype(jnp.float32)
            target[section, half, :, :, at] = product.astype(jnp.bfloat16)
            return c

        lax.fori_loop(0, half_width // tile, one_tile, 0)

    def pair_copy(section, half):
        return pltpu.make_async_remote_copy(
            src_ref=pair_out.at[section, half], dst_ref=pair_in.at[section, half],
            send_sem=pair_send.at[section, half], recv_sem=pair_recv.at[section, half],
            device_id={"cp": sibling}, device_id_type=MESH,
        )

    def mate_copy(section, half, k):
        to = (pair + k) % pairs
        return pltpu.make_async_remote_copy(
            src_ref=sums.at[section, half, to], dst_ref=mate_in.at[section, half, pair],
            send_sem=mate_send.at[section, half, to], recv_sem=mate_recv.at[section, half, pair],
            device_id={"cp": 2 * to + core}, device_id_type=MESH,
        )

    def wait_mate(section, half, k):
        src = (pair + pairs - k) % pairs
        pltpu.make_async_remote_copy(
            src_ref=mate_in.at[section, half, src], dst_ref=mate_in.at[section, half, src],
            send_sem=mate_send.at[section, half, src], recv_sem=mate_recv.at[section, half, src],
            device_id={"cp": 2 * src + core}, device_id_type=MESH,
        ).wait_recv()

    def total_of(section, half):
        total = sums[section, half, pair].astype(jnp.float32)
        for k in range(1, pairs):
            wait_mate(section, half, k)
            total += mate_in[section, half, (pair + pairs - k) % pairs].astype(jnp.float32)
        return total.astype(jnp.bfloat16)

    def to_sibling(section, half):
        if half == 0:
            gather_heads(section, 1 - core)
        project(section, half, 1 - core, pair_out, None)
        pair_copy(section, half).start()

    def to_mates(section, half):
        if half == 0:
            gather_heads(section, core)
        pair_copy(section, half).wait_recv()
        project(section, half, core, sums, pair_in)
        for k in range(1, pairs):
            mate_copy(section, half, k).start()

    order = [(other, 0), (other, 1), (sec, 0), (sec, 1)]
    to_sibling(*order[0])
    for n, spot in enumerate(order):
        if n + 1 < len(order):
            to_sibling(*order[n + 1])
        to_mates(*spot)

    homes = []
    for half in range(2):
        over[half] = total_of(other, half)
        home = pltpu.make_async_remote_copy(
            src_ref=over.at[half],
            dst_ref=out_ref.at[sec, :, pl.ds(half * half_width, half_width)],
            send_sem=home_send.at[half], recv_sem=home_recv.at[half],
            device_id={"section": other}, device_id_type=MESH,
        )
        home.start()
        homes.append(home)
    for half in range(2):
        out_ref[sec, :, half * half_width:(half + 1) * half_width] = total_of(sec, half)
    for home in homes:
        home.wait()
    for section, half in order:
        pair_copy(section, half).wait_send()
        for k in range(1, pairs):
            mate_copy(section, half, k).wait_send()

    def finish(i, carry):
        for way in range(2):
            place = last - tp if way == 0 else tp
            onward = tp - 1 if way == 0 else tp + 1
            back = tp + 1 if way == 0 else tp - 1
            head = way * per_way + i

            @pl.when(place < last)
            def _():
                for piece in range(pieces):
                    part_copy(head, piece, onward).wait_send()

            @pl.when(place > 0)
            def _():
                for r in range(att_pieces):
                    att_copy(head, r, back).wait_send()

        return carry

    lax.fori_loop(0, per_way, finish, 0)
    for copy in sent + square_copies:
        copy.wait_send()


def on_device(rollout_rows, lengths, block_owner, norm_gain, w_qkv, w_out):
    n_tp, n_cp, n_sec = lax.axis_size("tp"), lax.axis_size("cp"), lax.axis_size("section")
    own_rows, width = rollout_rows.shape
    blocks = n_sec * n_cp
    tokens = own_rows * blocks
    columns = w_qkv.shape[3]
    heads = columns // HEAD
    bf16, f32 = jnp.bfloat16, jnp.float32
    sends = 2 + 2 * n_cp
    vmem = pl.BlockSpec(memory_space=pltpu.VMEM)
    smem = pl.BlockSpec(memory_space=pltpu.SMEM)
    dma = pltpu.SemaphoreType.DMA
    pairs = n_cp // 2
    pieces = n_sec * pairs
    att_pieces = tokens // min(tokens, 256)
    exchange = pltpu.VMEM((n_sec, 2, pairs, own_rows, width // 2), bf16)
    return pl.pallas_call(
        functools.partial(attend_kernel, n_sec, n_cp, n_tp),
        out_shape=jax.ShapeDtypeStruct((n_sec, own_rows, width), bf16),
        in_specs=[vmem, vmem, smem, smem] + [pl.BlockSpec(memory_space=pl.ANY)] * 2,
        out_specs=vmem,
        scratch_shapes=[
            pltpu.VMEM((heads, blocks, own_rows, HEAD), bf16),
            pltpu.VMEM((columns, width), bf16),
            pltpu.VMEM((n_sec, 2, pairs * own_rows, columns), bf16),
            exchange,
            exchange,
            exchange,
            exchange,
            pltpu.VMEM((2, own_rows, width // 2), bf16),
            pltpu.VMEM((blocks, own_rows, width), bf16),
            pltpu.VMEM((blocks, own_rows, width), bf16),
            pltpu.VMEM((heads, width, 3 * HEAD), bf16),
            pltpu.VMEM((heads, tokens, 3 * HEAD), bf16),
            pltpu.VMEM((2 * own_rows, 3 * HEAD), f32),
            pltpu.VMEM((blocks, own_rows, HEAD), f32),
            pltpu.VMEM((n_tp, 8, tokens), f32),
            pltpu.VMEM((tokens, HEAD), f32),
            pltpu.VMEM((tokens, HEAD), bf16),
            pltpu.VMEM((tokens, HEAD), bf16),
            pltpu.VMEM((tokens, 1), jnp.int32),
            pltpu.VMEM((tokens, 1), jnp.int32),
            pltpu.VMEM((1, tokens), jnp.int32),
            dma((heads, 3)),
            dma((sends,)),
            dma((blocks,)),
            dma((n_tp,)),
            dma((n_tp,)),
            dma((heads, pieces)),
            dma((heads, pieces)),
            dma((heads, att_pieces)),
            dma((heads, att_pieces)),
            dma,
            dma((n_sec, 2)),
            dma((n_sec, 2)),
            dma((n_sec, 2, pairs)),
            dma((n_sec, 2, pairs)),
            dma((2,)),
            dma((2,)),
        ],
        compiler_params=pltpu.CompilerParams(
            collective_id=0, has_side_effects=True, vmem_limit_bytes=62 * 1024 * 1024
        ),
        name="attend",
    )(rollout_rows, norm_gain, block_owner, lengths, w_qkv, w_out)


def solution(mesh):
    return jax.shard_map(
        on_device,
        mesh=mesh,
        in_specs=(
            P(("section", "cp"), "tp"),
            P(),
            P(),
            P("section", "tp"),
            P("section", None, "tp", "cp"),
            P("section", "cp", "tp"),
        ),
        out_specs=P(None, ("section", "cp"), "tp"),
        check_vma=False,
    )
```
